128 devices in a mesh: head: 8 (over x, core), code: 16 (over y, z).
Axes of the slice: x: 4, y: 4, z: 4, core: 2. Of those that a mesh axis runs over, the one named last changes fastest.
Arguments:
- tokens: bfloat16 [16384, 1024], P(('head', 'code')), may hold values from -128 to 128
- codebook: bfloat16 [8, 32768, 128], P('head', 'code'), may hold values from -12.5 to 12.5
- ema_counts: float32 [8, 32768], P('head', 'code'), may hold values from 0.5 to 4
- ema_sums: float32 [8, 32768, 128], P('head', 'code'), may hold values from -6 to 6
Outputs:
- quantized: bfloat16 [16384, 1024], P(('head', 'code'))
- new_counts: float32 [8, 32768], P('head', 'code')
- new_codebook: float32 [8, 32768, 128], P('head', 'code')
The draws below stay inside these ranges and needn't reach their ends.
All inputs are finite; a program needn't handle non-finite values.
Results may differ from the reference program's by a relative error of at most 0.013.
Values may be sent and summed in bfloat16 or wider, within the bound.
A program may use at most 128 MiB of HBM per device.

```python
import math
import jax
import jax.numpy as jnp
from jax import lax

HD = 128
CODES_DEV = 2048
HEADS = 8
D = 1024
CODES = 32768
TOKENS = 16384


def code_offsets(key):
    key = jax.random.fold_in(key, 23)
    sign_key, size_key = jax.random.split(key, 2)
    sign_flips = 2.0 * jax.random.bernoulli(sign_key, 0.5, (HEADS, HD)).astype(jnp.float32) - 1.0
    magnitudes = jax.random.uniform(size_key, (HEADS, HD), jnp.float32, 1.0, 2.0)
    return sign_flips * magnitudes


def draw_tokens(key, part):
    base_key = key
    key = jax.random.fold_in(key, 7)
    scale_key, value_key, mix_key = jax.random.split(key, 3)
    scales = jnp.exp(jax.random.uniform(scale_key, (TOKENS, 1), jnp.float32, 0.0, math.log(10.0)))
    values = 0.3 * scales * jnp.clip(jax.random.normal(value_key, (TOKENS, D), jnp.float32), -5.0, 5.0)
    mixing = jax.random.uniform(mix_key, (TOKENS, HEADS, 1), jnp.float32, 0.42, 0.53)
    values = values + (mixing * code_offsets(base_key)[None, :, :]).reshape(TOKENS, D)
    return values.astype(jnp.bfloat16)


def draw_codebook(key, part):
    base_key = key
    key = jax.random.fold_in(key, 11)
    scale_key, value_key = jax.random.split(key, 2)
    scales = jnp.exp(jax.random.uniform(scale_key, (HEADS, CODES, 1), jnp.float32, 0.0, math.log(10.0)))
    values = 0.3 * scales * jnp.clip(jax.random.normal(value_key, (HEADS, CODES, HD), jnp.float32), -3.0, 3.0)
    offset_mask = (jnp.arange(CODES) >= CODES_DEV).astype(jnp.float32)
    values = values + offset_mask[None, :, None] * code_offsets(base_key)[:, None, :]
    return values.astype(jnp.bfloat16)


def levels(stream_key, extent, cuts, least, high):
    gain = 1.0
    for position, parts in cuts:
        draws = jax.random.uniform(jax.random.fold_in(jax.random.fold_in(stream_key, 6), position), (parts,), jnp.float32, least / len(cuts), high / len(cuts))
        gain = gain * jnp.repeat(jnp.exp(draws), extent[position] // parts).reshape((-1,) + (1,) * (len(extent) - 1 - position))
    return gain


def bell_draw(stream_key, shape, spread, reach, cuts=(), kind=jnp.bfloat16):
    values = jax.random.normal(stream_key, shape, jnp.float32) * spread
    if len(cuts) > 0:
        values = levels(stream_key, shape, cuts, -0.22, 0.18) * values
    return jnp.clip(values, min=-reach, max=reach).astype(kind)


def setup_inputs(seed: int = 0) -> dict:
    streams_of = jax.random.split(jax.random.key(seed), 5)
    return {
        "tokens": draw_tokens(jax.random.fold_in(streams_of[4], 71), 0),
        "codebook": draw_codebook(jax.random.fold_in(streams_of[4], 71), 0),
        "ema_counts": jnp.clip(jnp.exp(math.log(4.0) - 2.0794415 * jax.random.uniform(streams_of[2], (HEADS, CODES), jnp.float32) ** levels(streams_of[2], (HEADS, CODES), ((0, 8), (1, 16)), -0.2, 0.2)), 0.5, 4.0),
        "ema_sums": bell_draw(streams_of[3], (HEADS, CODES, HD), 1.0, 6.0, ((0, 8), (1, 16)), jnp.float32),
    }


sharpness = 0.25
momentum = 0.8


def reference(tokens, codebook, ema_counts, ema_sums):
    all_rows = tokens.shape[0]
    head_total = codebook.shape[0]
    code_total = codebook.shape[1]
    head_width = codebook.shape[2]
    block_rows = min(4096, all_rows)
    shard_total = code_total // CODES_DEV
    quant_pieces = []
    count_pieces = []
    numer_pieces = []
    for head_number in range(head_total):
        head_rows = tokens[:, head_number * head_width:(head_number + 1) * head_width]
        centroids = codebook[head_number]
        code_norms = jnp.sum(jnp.square(centroids.astype(jnp.float32)), axis=1)

        def advance(carried, block):
            assigned, numerators = carried
            products = jnp.dot(block, centroids.T, preferred_element_type=jnp.float32)
            logits = sharpness * (2.0 * products - code_norms[None, :])
            softmax_out = jax.nn.softmax(logits, axis=1)
            weights = softmax_out.astype(jnp.bfloat16)

            def shard_add(total, shard_number):
                start = (shard_number * CODES_DEV).astype(jnp.int32)
                weight_cols = lax.dynamic_slice_in_dim(weights, start, CODES_DEV, 1)
                code_rows = lax.dynamic_slice_in_dim(centroids, start, CODES_DEV, 0)
                partial_rows = jnp.dot(weight_cols, code_rows, preferred_element_type=jnp.float32)
                partial_rows = lax.optimization_barrier(partial_rows.astype(jnp.bfloat16))
                return total + partial_rows.astype(jnp.float32), None

            quant_total, _ = lax.scan(shard_add, jnp.zeros((block.shape[0], head_width), jnp.float32), jnp.arange(shard_total, dtype=jnp.int32))
            quant_block = quant_total.astype(jnp.bfloat16)
            assigned = assigned + jnp.sum(softmax_out, axis=0)
            numerators = numerators + jnp.dot(weights.T, block, preferred_element_type=jnp.float32)
            return (assigned, numerators), quant_block

        start_state = (jnp.zeros((code_total,), jnp.float32), jnp.zeros((code_total, head_width), jnp.float32))
        blocks = head_rows.reshape(all_rows // block_rows, block_rows, head_width)
        (assigned, numerators), quant_blocks = lax.scan(advance, start_state, blocks)
        quant_pieces.append(quant_blocks.reshape(all_rows, head_width))
        count_pieces.append(assigned)
        numer_pieces.append(numerators)
    quantized = jnp.concatenate(quant_pieces, axis=1)
    assigned_all = jnp.stack(count_pieces, axis=0)
    numer_all = jnp.stack(numer_pieces, axis=0)
    new_counts = momentum * ema_counts + (1.0 - momentum) * assigned_all
    new_sums = momentum * ema_sums + (1.0 - momentum) * numer_all
    new_codebook = new_sums / new_counts[:, :, None]
    return quantized, new_counts, new_codebook
```

```python
import functools

import jax
import jax.numpy as jnp
from jax import lax
from jax.experimental import pallas as pl
from jax.experimental.pallas import tpu as pltpu
from jax.sharding import PartitionSpec as P

MESH = pl.DeviceIdType.MESH
bf16 = jnp.bfloat16
f32 = jnp.float32
momentum = 0.8
half_log2e = 0.5 * 1.4426950408889634
RING = 4
QROWS = 144


def dot(a, b, ca, cb):
    return lax.dot_general(a, b, (((ca,), (cb,)), ((), ())), preferred_element_type=f32)


def gray(s):
    return s + (s // 2) * (1 - 2 * (s % 2))


def kernel(
    heads, tok_ref, cb_ref, cnt_ref, sums_hbm,
    quant_ref, ncnt_ref, ncb_ref, spill,
    e_buf, s_buf, m_buf, c_land, naug, c_t, tsend, x_land, q_acc, stat, stat_land, mloc, f_buf,
    qsend, qland, osend, oland, nsend, nland, ksend, kland,
    e_sem, sums_sem, c_ss, c_rs, h_ss, h_rs, y_ss, y_rs, st_ss, st_rs, q_ss, q_rs, o_ss, o_rs, n_ss, n_rs, k_ss, k_rs,
):
    h = lax.axis_index("head")
    code = lax.axis_index("code")
    y, z = code // RING, code % RING
    width = tok_ref.shape[0]
    codes, hd = cb_ref.shape[1], cb_ref.shape[2]
    tile = x_land.shape[2] // 2

    def at_head(d):
        return (lax.rem(h + d, heads), code)

    def at_y(d):
        return (h, lax.rem(y + d, RING) * RING + z)

    def at_z(d):
        return (h, y * RING + lax.rem(z + d, RING))

    def remote(src, dst, ss, rs, where):
        return pltpu.make_async_remote_copy(
            src_ref=src, dst_ref=dst, send_sem=ss, recv_sem=rs, device_id=where, device_id_type=MESH
        )

    sums_buf = s_buf.at[1, :, pl.ds(0, hd)]

    def sum_copy():
        return pltpu.make_async_copy(sums_hbm.at[0], sums_buf, sums_sem)

    barrier = pltpu.get_barrier_semaphore()
    for d in range(1, heads):
        pl.semaphore_signal(barrier, inc=1, device_id=at_head(d), device_id_type=MESH)
    for d in range(1, RING):
        pl.semaphore_signal(barrier, inc=1, device_id=at_y(d), device_id_type=MESH)
        pl.semaphore_signal(barrier, inc=1, device_id=at_z(d), device_id_type=MESH)
    for g in range(heads):
        block = tok_ref[:, g * hd:(g + 1) * hd].astype(f32)
        tsend[g] = jnp.transpose(block).astype(bf16)
    pl.semaphore_wait(barrier, heads - 1 + 2 * (RING - 1))

    def head_copy(d):
        return remote(
            tsend.at[lax.rem(h + d, heads)],
            x_land.at[y, :, pl.ds(pl.multiple_of(h * width, 128), width)],
            h_ss.at[d - 1], h_rs.at[d - 1], at_head(d),
        )

    def c_copy(d):
        return remote(cb_ref.at[0], c_land.at[z], c_ss.at[d - 1], c_rs.at[d - 1], at_z(d))

    def y_copy(d):
        return remote(x_land.at[y], x_land.at[y], y_ss.at[d - 1], y_rs.at[d - 1], at_y(d))

    for d in range(1, heads):
        head_copy(d).start()
    for d in (1, 3, 2):
        c_copy(d).start()
    x_land[y, :, pl.ds(pl.multiple_of(h * width, 128), width)] = tsend[h]
    c_land[z] = cb_ref[0]

    for slot in range(2):
        lane = lax.broadcasted_iota(jnp.int32, (QROWS - hd, codes), 0)
        c_t[slot, hd:, :] = jnp.where(lane == 0, 1.0, 0.0).astype(bf16)
    row = lax.broadcasted_iota(jnp.int32, (hd, tile), 0)
    ones_rows = jnp.where(row < 3, 1.0, 0.0).astype(bf16)

    def prepare(slot, zb):
        c = c_land[zb].astype(f32)
        n = -0.5 * jnp.sum(c * c, axis=1, keepdims=True)
        hi = n.astype(bf16).astype(f32)
        rest = n - hi
        mid = rest.astype(bf16).astype(f32)
        low = rest - mid
        lane = lax.broadcasted_iota(jnp.int32, (codes, hd), 1)
        naug[slot] = jnp.where(lane == 0, hi, jnp.where(lane == 1, mid, jnp.where(lane == 2, low, 0.0))).astype(bf16)
        c_t[slot, 0:hd, :] = jnp.transpose(c).astype(bf16)

    prepare(0, z)
    stat[0] = jnp.full(stat.shape[1:], -3e38, f32)
    q_acc[...] = jnp.zeros(q_acc.shape, f32)

    for d in range(1, heads):
        head_copy(d).wait()
    for d in (1, 3, 2):
        y_copy(d).start()

    def logits(j, s, half, slot):
        zb = lax.rem(z + gray(j), RING)
        yb = lax.rem(y + gray(s), RING)
        left = jnp.concatenate([c_land[zb], naug[j % 2]], axis=1)
        right = jnp.concatenate([x_land[yb, :, half * tile:(half + 1) * tile], ones_rows], axis=0)
        out = dot(left, right, 1, 0)
        s_buf[slot] = out
        m_buf[slot] = jnp.max(out, axis=0, keepdims=True)

    def finish(j, s, half, slot):
        ta = 2 * lax.rem(y + gray(s), RING) + half
        es = (j % 2) * (2 * RING) + 2 * s + half
        m = m_buf[slot]
        e = jnp.exp2((s_buf[slot] - m) * half_log2e).astype(bf16)
        e_buf[es] = e
        q = dot(c_t[j % 2], e, 1, 0)
        m_old = stat[0, pl.ds(ta, 1), :]
        m_new = jnp.maximum(m_old, m)
        q_acc[ta] = q_acc[ta] * jnp.exp2((m_old - m_new) * half_log2e) + q * jnp.exp2((m - m_new) * half_log2e)
        stat[0, pl.ds(ta, 1), :] = m_new
        mloc[j, pl.ds(ta, 1), :] = m

    def spill_copy(es):
        return pltpu.make_async_copy(e_buf.at[es], spill.at[es], e_sem.at[es])

    def fetch_copy(es):
        return pltpu.make_async_copy(spill.at[es], e_buf.at[es], e_sem.at[es])

    pairs = RING * RING
    logits(0, 0, 0, 0)

    def step(p, _):
        j, s = p // RING, p % RING
        pn = (p + 1) % pairs
        jn, sn = pn // RING, pn % RING
        es = (j % 2) * (2 * RING) + 2 * s

        @pl.when(p < RING - 1)
        def _():
            o = gray(p + 1)
            src = lax.rem(y + o, RING)
            remote(x_land.at[src], x_land.at[src], y_ss.at[3 - o], y_rs.at[3 - o], at_y(4 - o)).wait_recv()

        @pl.when((s == RING - 1) & (j < RING - 1))
        def _():
            o = gray(j + 1)
            src = lax.rem(z + o, RING)
            remote(cb_ref.at[0], c_land.at[src], c_ss.at[3 - o], c_rs.at[3 - o], at_z(4 - o)).wait_recv()
            prepare(jn % 2, src)

        @pl.when(j >= 2)
        def _():
            spill_copy(es).wait()
            spill_copy(es + 1).wait()

        logits(j, s, 1, 1)
        finish(j, s, 0, 0)
        logits(jn, sn, 0, 0)
        finish(j, s, 1, 1)

        @pl.when(j < 2)
        def _():
            spill_copy(es).start()
            spill_copy(es + 1).start()

        return 0

    lax.fori_loop(0, pairs, step, 0)
    sum_copy().start()

    for t in range(2 * RING):
        stat[1, t:t + 1, :] = q_acc[t, hd:hd + 1, :]

    def stat_copy(d):
        return remote(stat, stat_land.at[d - 1], st_ss.at[d - 1], st_rs.at[d - 1], at_y(d))

    for d in range(1, RING):
        stat_copy(d).start()
    for d in range(1, RING):
        stat_copy(d).wait()
    top = stat[0]
    for d in range(1, RING):
        top = jnp.maximum(top, stat_land[d - 1, 0])
    total = stat[1] * jnp.exp2((stat[0] - top) * half_log2e)
    for d in range(1, RING):
        total = total + stat_land[d - 1, 1] * jnp.exp2((stat_land[d - 1, 0] - top) * half_log2e)
    inverse = 1.0 / total
    for j in range(RING):
        f_buf[j] = jnp.exp2((mloc[j] - top) * half_log2e) * inverse
    gain = jnp.exp2((stat[0] - top) * half_log2e) * inverse
    for t in range(2 * RING):
        qsend[t // 2, :, (t % 2) * tile:(t % 2 + 1) * tile] = (q_acc[t, 0:hd, :] * gain[t:t + 1, :]).astype(bf16)

    def q_copy(d):
        return remote(
            qsend.at[lax.rem(y + d, RING)], qland.at[d - 1], q_ss.at[d - 1], q_rs.at[d - 1], at_y(d)
        )

    for d in (2, 1, 3):
        q_copy(d).start()

    def o_copy(d):
        return remote(osend.at[lax.rem(h + d, heads)], oland.at[h], o_ss.at[d - 1], o_rs.at[d - 1], at_head(d))

    def send_quantized():
        for d in range(1, RING):
            q_copy(d).wait()
        for g in range(heads):
            cols = slice(g * width, (g + 1) * width)
            block = qsend[y, :, cols].astype(f32)
            for d in range(1, RING):
                block = block + qland[d - 1, :, cols].astype(f32)
            osend[g] = jnp.transpose(block).astype(bf16)
        for d in range(1, heads):
            o_copy(d).start()
        oland[h] = osend[h]

    group = 4
    acc = s_buf.at[0]
    pad_row = lax.broadcasted_iota(jnp.int32, (hd, tile), 0)

    def n_copy(jj, d):
        return remote(nsend.at[jj], nland.at[d - 1], n_ss.at[d - 1], n_rs.at[d - 1], at_z(d))

    def k_copy(jj, d):
        return remote(ksend.at[jj], kland.at[d - 1], k_ss.at[d - 1], k_rs.at[d - 1], at_z(d))

    count_row = None
    for jj in range(RING):
        j = RING - 1 - jj
        base = (j % 2) * (2 * RING)

        def partial_sums(g, _, j=j, jj=jj, base=base):
            lefts, rights = [], []
            if jj >= 2:
                for u in range(group):
                    fetch_copy(base + group * g + u).wait()
            for u in range(group):
                s = (group // 2) * g + u // 2
                yb = lax.rem(y + gray(s), RING)
                ta = 2 * yb + u % 2
                f = f_buf[j, pl.ds(ta, 1), :]
                x = x_land[yb, :, (u % 2) * tile:(u % 2 + 1) * tile].astype(f32)
                f_hi = f.astype(bf16).astype(f32)
                extra = jnp.where(pad_row == 0, f_hi, jnp.where(pad_row == 1, f - f_hi, 0.0))
                rights.append(jnp.concatenate([(x * f).astype(bf16), extra.astype(bf16)], axis=0))
                lefts.append(e_buf[base + group * g + u])
            part = dot(jnp.concatenate(lefts, axis=1), jnp.concatenate(rights, axis=1), 1, 1)
            acc[:, 0:2 * hd] = acc[:, 0:2 * hd] + part
            if jj < 2:
                for u in range(group):
                    fetch_copy(base + group * g + u).start()
            return 0

        acc[:, 0:2 * hd] = jnp.zeros((codes, 2 * hd), f32)
        lax.fori_loop(0, 2 * RING // group, partial_sums, 0)
        counts = jnp.transpose(acc[:, hd:2 * hd])
        count_row = counts[0:1, :] + counts[1:2, :]
        if j > 0:
            d = (2, 3, 1)[jj]
            nsend[jj] = acc[:, 0:hd].astype(bf16)
            ksend[jj] = jnp.broadcast_to(count_row, ksend.shape[1:])
            n_copy(jj, d).start()
            k_copy(jj, d).start()
        if jj == 0:
            send_quantized()

    for jj, d in enumerate((2, 3, 1)):
        n_copy(jj, d).wait()
        k_copy(jj, d).wait()
    sum_copy().wait()
    for d in range(1, RING):
        count_row = count_row + kland[d - 1, 0:1, :]
    new_counts = momentum * cnt_ref[...] + (1.0 - momentum) * count_row
    ncnt_ref[...] = new_counts
    inverse_counts = jnp.transpose(jnp.broadcast_to(1.0 / new_counts, (8, codes)))[:, 0:1]
    numerators = acc[:, 0:hd]
    for d in range(1, RING):
        numerators = numerators + nland[d - 1].astype(f32)
    ncb_ref[0] = (momentum * sums_buf[...] + (1.0 - momentum) * numerators) * inverse_counts

    for d in range(1, heads):
        o_copy(d).wait()
    for g in range(heads):
        quant_ref[:, g * hd:(g + 1) * hd] = oland[g]
    for d in (1, 3, 2):
        c_copy(d).wait_send()
        y_copy(d).wait_send()


def shards(tokens, codebook, ema_counts, ema_sums):
    heads = lax.axis_size("head")
    width, _ = tokens.shape
    _, codes, hd = codebook.shape
    rows = heads * width
    tile = rows // 2
    vmem = pl.BlockSpec(memory_space=pltpu.VMEM)
    dma = pltpu.SemaphoreType.DMA
    anywhere = pl.BlockSpec(memory_space=pl.ANY)
    far = RING - 1
    quantized, counts, book, _ = pl.pallas_call(
        functools.partial(kernel, heads),
        out_shape=(
            jax.ShapeDtypeStruct(tokens.shape, bf16),
            jax.ShapeDtypeStruct(ema_counts.shape, f32),
            jax.ShapeDtypeStruct(ema_sums.shape, f32),
            jax.ShapeDtypeStruct((4 * RING, codes, tile), bf16),
        ),
        in_specs=[vmem, vmem, vmem, anywhere],
        out_specs=(vmem, vmem, vmem, anywhere),
        scratch_shapes=[
            pltpu.VMEM((4 * RING, codes, tile), bf16),
            pltpu.VMEM((2, codes, tile), f32),
            pltpu.VMEM((2, 1, tile), f32),
            pltpu.VMEM((RING, codes, hd), bf16),
            pltpu.VMEM((2, codes, hd), bf16),
            pltpu.VMEM((2, QROWS, codes), bf16),
            pltpu.VMEM((heads, hd, width), bf16),
            pltpu.VMEM((RING, hd, rows), bf16),
            pltpu.VMEM((2 * RING, QROWS, tile), f32),
            pltpu.VMEM((2, 2 * RING, tile), f32),
            pltpu.VMEM((far, 2, 2 * RING, tile), f32),
            pltpu.VMEM((RING, 2 * RING, tile), f32),
            pltpu.VMEM((RING, 2 * RING, tile), f32),
            pltpu.VMEM((RING, hd, rows), bf16),
            pltpu.VMEM((far, hd, rows), bf16),
            pltpu.VMEM((heads, width, hd), bf16),
            pltpu.VMEM((heads, width, hd), bf16),
            pltpu.VMEM((far, codes, hd), bf16),
            pltpu.VMEM((far, codes, hd), bf16),
            pltpu.VMEM((far, 8, codes), f32),
            pltpu.VMEM((far, 8, codes), f32),
            dma((4 * RING,)),
            dma,
            dma((far,)), dma((far,)),
            dma((max(heads - 1, 1),)), dma((max(heads - 1, 1),)),
            dma((far,)), dma((far,)),
            dma((far,)), dma((far,)),
            dma((far,)), dma((far,)),
            dma((max(heads - 1, 1),)), dma((max(heads - 1, 1),)),
            dma((far,)), dma((far,)),
            dma((far,)), dma((far,)),
        ],
        compiler_params=pltpu.CompilerParams(
            collective_id=0, has_side_effects=True, vmem_limit_bytes=63 * 2**20
        ),
    )(tokens, codebook, ema_counts, ema_sums)
    return quantized, counts, book


def solution(mesh):
    placed = (
        P(("head", "code"), None),
        P("head", "code", None),
        P("head", "code"),
        P("head", "code", None),
    )
    return jax.shard_map(
        shards,
        mesh=mesh,
        in_specs=placed,
        out_specs=(P(("head", "code"), None), P("head", "code"), P("head", "code", None)),
        check_vma=False,
    )
```

```python
import functools

import jax
import jax.numpy as jnp
from jax import lax
from jax.experimental import pallas as pl
from jax.experimental.pallas import tpu as pltpu
from jax.sharding import PartitionSpec as P

MESH = pl.DeviceIdType.MESH
bf16 = jnp.bfloat16
f32 = jnp.float32
momentum = 0.8
half_log2e = 0.5 * 1.4426950408889634
RING = 4
QROWS = 144


def dot(a, b, ca, cb):
    return lax.dot_general(a, b, (((ca,), (cb,)), ((), ())), preferred_element_type=f32)


def gray(s):
    return s + (s // 2) * (1 - 2 * (s % 2))


def kernel(
    heads, tok_ref, cb_ref, cnt_ref, sums_hbm,
    oland, ncnt_ref, ncb_hbm, spill,
    e_buf, s_buf, m_buf, c_land, naug, c_t, naug_next, c_t_next, tsend, x_land, q_acc, stat, stat_land, mloc, f_buf,
    qsend, qland, nsend, nland, ksend, kland,
    e_sem, sums_sem, own_sem, book_sem, c_ss, c_rs, h_ss, h_rs, y_ss, y_rs, st_ss, st_rs, q_ss, q_rs, o_ss, o_rs, n_ss, n_rs, k_ss, k_rs,
):
    h = lax.axis_index("head")
    code = lax.axis_index("code")
    y, z = code // RING, code % RING
    width = tok_ref.shape[0]
    codes, hd = cb_ref.shape[1], cb_ref.shape[2]
    tile = x_land.shape[2] // 2

    def at_head(d):
        return (lax.rem(h + d, heads), code)

    def at_y(d):
        return (h, lax.rem(y + d, RING) * RING + z)

    def at_z(d):
        return (h, y * RING + lax.rem(z + d, RING))

    def remote(src, dst, ss, rs, where):
        return pltpu.make_async_remote_copy(
            src_ref=src, dst_ref=dst, send_sem=ss, recv_sem=rs, device_id=where, device_id_type=MESH
        )

    sums_buf = s_buf.at[1, :, pl.ds(0, hd)]

    def sum_copy():
        return pltpu.make_async_copy(sums_hbm.at[0], sums_buf, sums_sem)

    barrier = pltpu.get_barrier_semaphore()
    for d in range(1, heads):
        pl.semaphore_signal(barrier, inc=1, device_id=at_head(d), device_id_type=MESH)
    for d in range(1, RING):
        pl.semaphore_signal(barrier, inc=1, device_id=at_y(d), device_id_type=MESH)
        pl.semaphore_signal(barrier, inc=1, device_id=at_z(d), device_id_type=MESH)
    for g in range(heads):
        block = tok_ref[:, g * hd:(g + 1) * hd].astype(f32)
        tsend[g] = jnp.transpose(block).astype(bf16)
    pl.semaphore_wait(barrier, heads - 1 + 2 * (RING - 1))

    def head_copy(d):
        return remote(
            tsend.at[lax.rem(h + d, heads)],
            x_land.at[y, :, pl.ds(pl.multiple_of(h * width, 128), width)],
            h_ss.at[d - 1], h_rs.at[d - 1], at_head(d),
        )

    def c_copy(d):
        return remote(cb_ref.at[0], c_land.at[z], c_ss.at[d - 1], c_rs.at[d - 1], at_z(d))

    def y_copy(d, half):
        block = x_land.at[y, :, pl.ds(half * tile, tile)]
        return remote(block, block, y_ss.at[half, d - 1], y_rs.at[half, d - 1], at_y(d))

    for d in range(1, heads):
        head_copy(d).start()
    for d in (1, 3):
        c_copy(d).start()
    x_land[y, :, pl.ds(pl.multiple_of(h * width, 128), width)] = tsend[h]
    c_land[z] = cb_ref[0]

    tail = lax.broadcasted_iota(jnp.int32, (QROWS - hd, codes), 0)
    for slot in range(2):
        c_t[slot, hd:, :] = jnp.where(tail == 0, 1.0, 0.0).astype(bf16)
    row = lax.broadcasted_iota(jnp.int32, (hd, tile), 0)
    ones_rows = jnp.where(row < 3, 1.0, 0.0).astype(bf16)

    def prepare(aug, cols, zb, start, count):
        part = pl.ds(start, count)
        c = c_land[zb, part, :].astype(f32)
        n = -0.5 * jnp.sum(c * c, axis=1, keepdims=True)
        hi = n.astype(bf16).astype(f32)
        rest = n - hi
        mid = rest.astype(bf16).astype(f32)
        low = rest - mid
        lane = lax.broadcasted_iota(jnp.int32, (count, hd), 1)
        aug[part, :] = jnp.where(lane == 0, hi, jnp.where(lane == 1, mid, jnp.where(lane == 2, low, 0.0))).astype(bf16)
        cols[0:hd, part] = jnp.transpose(c).astype(bf16)

    prepare(naug.at[0], c_t.at[0], z, 0, codes)
    stat[...] = jnp.full(stat.shape, -3e38, f32)
    q_acc[...] = jnp.zeros(q_acc.shape, f32)

    for d in range(1, heads):
        head_copy(d).wait()
    for half in range(2):
        for d in (1, 3):
            y_copy(d, half).start()

    def row_block(j, s):
        first = 1 - (j + 3) // 4
        return lax.rem(first * (y + gray(s)) + (1 - first) * s, RING)

    def logits(j, s, half, slot):
        zb = lax.rem(z + gray(j), RING)
        yb = row_block(j, s)
        left = jnp.concatenate([c_land[zb], naug[j % 2]], axis=1)
        right = jnp.concatenate([x_land[yb, :, half * tile:(half + 1) * tile], ones_rows], axis=0)
        out = dot(left, right, 1, 0)
        s_buf[slot] = out
        m_buf[slot] = jnp.max(out, axis=0, keepdims=True)

    def finish(j, s, half, slot):
        yb = row_block(j, s)
        es = (j % 2) * (2 * RING) + 2 * s + half
        m = m_buf[slot]
        e = jnp.exp2((s_buf[slot] - m) * half_log2e).astype(bf16)
        e_buf[es] = e
        q = dot(c_t[j % 2], e, 1, 0)
        m_old = stat[yb, half:half + 1, :]
        m_new = jnp.maximum(m_old, m)
        q = q_acc[2 * yb + half] * jnp.exp2((m_old - m_new) * half_log2e) + q * jnp.exp2((m - m_new) * half_log2e)
        q_acc[2 * yb + half] = q
        stat[yb, half:half + 1, :] = m_new
        stat[yb, 2 + half:3 + half, :] = q[hd:hd + 1, :]
        mloc[yb, pl.ds(2 * j + half, 1), :] = m

    def spill_copy(es):
        return pltpu.make_async_copy(e_buf.at[es], spill.at[es], e_sem.at[es])

    def fetch_copy(es):
        return pltpu.make_async_copy(spill.at[es], e_buf.at[es], e_sem.at[es])

    def wait_rows(s, half):
        o = gray(s)
        block = x_land.at[lax.rem(y + o, RING), :, pl.ds(half * tile, tile)]
        remote(block, block, y_ss.at[half, 3 - o], y_rs.at[half, 3 - o], at_y(4 - o)).wait_recv()

    def wait_codes(j):
        o = gray(j)
        remote(
            cb_ref.at[0], c_land.at[lax.rem(z + o, RING)], c_ss.at[3 - o], c_rs.at[3 - o], at_z(4 - o)
        ).wait_recv()

    def jn_of(j):
        return (j + 1) % RING

    def stat_copy(b, d):
        return remote(stat.at[b], stat_land.at[d - 1, b], st_ss.at[b, d - 1], st_rs.at[b, d - 1], at_y(d))

    pairs = RING * RING
    quarter = codes // RING
    logits(0, 0, 0, 0)

    def step(p, _):
        j, s = p // RING, p % RING
        pn = (p + 1) % pairs
        jn, sn = pn // RING, pn % RING
        es = (j % 2) * (2 * RING) + 2 * s

        @pl.when(p < RING - 1)
        def _():
            wait_rows(p + 1, 0)

        @pl.when((p > 0) & (p < RING))
        def _():
            wait_rows(p, 1)

        @pl.when(p == 1)
        def _():
            for half in range(2):
                for d in (1, 3):
                    y_copy(d, half).wait_send()
            for half in range(2):
                y_copy(2, half).start()

        @pl.when(p == 3)
        def _():
            for d in (1, 3):
                c_copy(d).wait_send()
            c_copy(2).start()
            wait_codes(1)
            prepare(naug.at[1], c_t.at[1], lax.rem(z + 1, RING), 0, codes)

        @pl.when((s == 0) & (j > 0) & (j < RING - 1))
        def _():
            wait_codes(j + 1)

        ahead = lax.rem(z + gray(jn_of(j)) * ((j + 3) // 4), RING)

        @pl.when((s == RING - 1) & (j > 0) & (j < RING - 1))
        def _():
            slot = jn_of(j) % 2
            done = (RING - 1) * quarter
            naug[slot, 0:done, :] = naug_next[0:done, :]
            c_t[slot, 0:hd, 0:done] = c_t_next[0:hd, 0:done]
            prepare(naug.at[slot], c_t.at[slot], ahead, done, quarter)

        @pl.when(j >= 2)
        def _():
            spill_copy(es).wait()
            spill_copy(es + 1).wait()

        logits(j, s, 1, 1)
        finish(j, s, 0, 0)
        logits(jn, sn, 0, 0)
        finish(j, s, 1, 1)
        prepare(naug_next, c_t_next, ahead, pl.multiple_of(s * quarter, quarter), quarter)

        @pl.when(j == RING - 1)
        def _():
            for d in range(1, RING):
                stat_copy(s, d).start()

        @pl.when(j < 2)
        def _():
            spill_copy(es).start()
            spill_copy(es + 1).start()

        return 0

    lax.fori_loop(0, pairs, step, 0)
    sum_copy().start()

    def q_copy(b):
        d = lax.rem(b - y + RING, RING)
        return remote(qsend.at[b], qland.at[d - 1], q_ss.at[d - 1], q_rs.at[d - 1], (h, b * RING + z))

    def q_wait(d):
        b = lax.rem(y + d, RING)
        return remote(qsend.at[b], qland.at[d - 1], q_ss.at[d - 1], q_rs.at[d - 1], (h, b * RING + z))

    def totals(b):
        for d in range(1, RING):
            stat_copy(b, d).wait()
        m, l = stat[b, 0:2, :], stat[b, 2:4, :]
        top = m
        for d in range(1, RING):
            top = jnp.maximum(top, stat_land[d - 1, b, 0:2, :])
        total = l * jnp.exp2((m - top) * half_log2e)
        for d in range(1, RING):
            total = total + stat_land[d - 1, b, 2:4, :] * jnp.exp2((stat_land[d - 1, b, 0:2, :] - top) * half_log2e)
        inverse = 1.0 / total
        gain = jnp.exp2((m - top) * half_log2e) * inverse
        even = lax.broadcasted_iota(jnp.int32, (2 * RING, tile), 0) % 2 == 0
        top_all = jnp.where(even, top[0:1, :], top[1:2, :])
        f_buf[b] = jnp.exp2((mloc[b] - top_all) * half_log2e) * jnp.where(even, inverse[0:1, :], inverse[1:2, :])
        for half in range(2):
            cols = slice(half * tile, (half + 1) * tile)
            qsend[b, :, cols] = (q_acc[2 * b + half, 0:hd, :] * gain[half:half + 1, :]).astype(bf16)

        @pl.when(y != b)
        def _():
            q_copy(b).start()

    def o_copy(d):
        return remote(tsend.at[lax.rem(h + d, heads)], oland.at[h], o_ss.at[d - 1], o_rs.at[d - 1], at_head(d))

    def send_quantized():
        for d in range(1, RING):
            q_wait(d).wait()
        for g in range(heads):
            cols = slice(g * width, (g + 1) * width)
            block = qsend[y, :, cols].astype(f32)
            for d in range(1, RING):
                block = block + qland[d - 1, :, cols].astype(f32)
            tsend[g] = jnp.transpose(block).astype(bf16)
        for d in range(1, heads):
            o_copy(d).start()
        pltpu.make_async_copy(tsend.at[h], oland.at[h], own_sem).start()

    group = 4
    half_codes = codes // 2
    acc = s_buf.at[0, :, pl.ds(0, 2 * hd)]
    pad_row = lax.broadcasted_iota(jnp.int32, (hd, tile), 0)

    def n_copy(jj, d, ch):
        part = pl.ds(pl.multiple_of(ch * half_codes, half_codes), half_codes)
        return remote(nsend.at[jj, part], nland.at[d - 1, part], n_ss.at[d - 1, ch], n_rs.at[d - 1, ch], at_z(d))

    def k_copy(jj, d, ch):
        part = pl.ds(pl.multiple_of(ch * half_codes, half_codes), half_codes)
        return remote(
            ksend.at[jj, :, part], kland.at[d - 1, :, part], k_ss.at[d - 1, ch], k_rs.at[d - 1, ch], at_z(d)
        )

    def scaled(j, t):
        yb = row_block(j, t // 2)
        f = f_buf[yb, 2 * j + t % 2:2 * j + t % 2 + 1, :]
        x = x_land[yb, :, (t % 2) * tile:(t % 2 + 1) * tile].astype(f32)
        f_hi = f.astype(bf16).astype(f32)
        extra = jnp.where(pad_row == 0, f_hi, jnp.where(pad_row == 1, f - f_hi, 0.0))
        return jnp.concatenate([(x * f).astype(bf16), extra.astype(bf16)], axis=0)

    routes = (2, 3, 1)
    for jj in range(RING):
        j = RING - 1 - jj
        base = (j % 2) * (2 * RING)
        for g in range(2 * RING // group):
            tiles = range(g * group, (g + 1) * group)
            if jj == 0:
                for b in range(g * group // 2, (g + 1) * group // 2):
                    totals(b)
            if jj >= 2:
                for t in tiles:
                    fetch_copy(base + t).wait()

            def some_codes(ch, _, j=j, jj=jj, base=base, tiles=tiles, g=g):
                part = pl.ds(pl.multiple_of(ch * half_codes, half_codes), half_codes)
                left = jnp.concatenate([e_buf[base + t, part, :] for t in tiles], axis=1)
                right = jnp.concatenate([scaled(j, t) for t in tiles], axis=1)
                out = dot(left, right, 1, 1)
                if g > 0:
                    out = out + acc[part, :]
                if g < 2 * RING // group - 1:
                    acc[part, :] = out
                else:
                    columns = jnp.transpose(out[:, hd:2 * hd])
                    row = columns[0:1, :] + columns[1:2, :]
                    ksend[jj, :, part] = jnp.broadcast_to(row, (8, half_codes))
                    if j > 0:
                        nsend[jj, part, :] = out[:, 0:hd].astype(bf16)
                        n_copy(jj, routes[jj], ch).start()
                        k_copy(jj, routes[jj], ch).start()
                    else:
                        acc[part, 0:hd] = out[:, 0:hd]
                return 0

            lax.fori_loop(0, 2, some_codes, 0)
            if jj < 2:
                for t in tiles:
                    fetch_copy(base + t).start()
        if jj == 2:
            send_quantized()

    sum_copy().wait()
    book_copies = []
    for ch in range(2):
        part = slice(ch * half_codes, (ch + 1) * half_codes)
        for jj, d in enumerate(routes):
            n_copy(jj, d, ch).wait()
            k_copy(jj, d, ch).wait()
        row = ksend[RING - 1, 0:1, part]
        numerators = acc[part, 0:hd]
        for d in range(1, RING):
            row = row + kland[d - 1, 0:1, part]
            numerators = numerators + nland[d - 1, part, :].astype(f32)
        new_counts = momentum * cnt_ref[:, part] + (1.0 - momentum) * row
        ncnt_ref[:, part] = new_counts
        inverse_counts = jnp.transpose(jnp.broadcast_to(1.0 / new_counts, (8, half_codes)))[:, 0:1]
        sums_buf[part, :] = (momentum * sums_buf[part, :] + (1.0 - momentum) * numerators) * inverse_counts
        book_copies.append(
            pltpu.make_async_copy(
                sums_buf.at[pl.ds(ch * half_codes, half_codes)],
                ncb_hbm.at[0, pl.ds(ch * half_codes, half_codes)],
                book_sem.at[ch],
            )
        )
        book_copies[-1].start()
    for d in range(1, heads):
        o_copy(d).wait()
    pltpu.make_async_copy(tsend.at[h], oland.at[h], own_sem).wait()
    c_copy(2).wait_send()
    for half in range(2):
        y_copy(2, half).wait_send()
    for copy in book_copies:
        copy.wait()


def place(oland, counts, book, quant_ref, ncnt_ref, ncb_ref):
    heads, _, hd = oland.shape
    for g in range(heads):
        quant_ref[:, g * hd:(g + 1) * hd] = oland[g]
    ncnt_ref[...] = counts[...]
    ncb_ref[...] = book[...]


def shards(tokens, codebook, ema_counts, ema_sums):
    heads = lax.axis_size("head")
    width, _ = tokens.shape
    _, codes, hd = codebook.shape
    rows = heads * width
    tile = rows // 2
    vmem = pl.BlockSpec(memory_space=pltpu.VMEM)
    dma = pltpu.SemaphoreType.DMA
    anywhere = pl.BlockSpec(memory_space=pl.ANY)
    far = RING - 1
    pieces, counts, book, _ = pl.pallas_call(
        functools.partial(kernel, heads),
        out_shape=(
            jax.ShapeDtypeStruct((heads, width, hd), bf16),
            jax.ShapeDtypeStruct(ema_counts.shape, f32),
            jax.ShapeDtypeStruct(ema_sums.shape, f32),
            jax.ShapeDtypeStruct((4 * RING, codes, tile), bf16),
        ),
        in_specs=[vmem, vmem, vmem, anywhere],
        out_specs=(anywhere, vmem, anywhere, anywhere),
        scratch_shapes=[
            pltpu.VMEM((4 * RING, codes, tile), bf16),
            pltpu.VMEM((2, codes, tile), f32),
            pltpu.VMEM((2, 1, tile), f32),
            pltpu.VMEM((RING, codes, hd), bf16),
            pltpu.VMEM((2, codes, hd), bf16),
            pltpu.VMEM((2, QROWS, codes), bf16),
            pltpu.VMEM((codes, hd), bf16),
            pltpu.VMEM((hd, codes), bf16),
            pltpu.VMEM((heads, hd, width), bf16),
            pltpu.VMEM((RING, hd, rows), bf16),
            pltpu.VMEM((2 * RING, QROWS, tile), f32),
            pltpu.VMEM((RING, 8, tile), f32),
            pltpu.VMEM((far, RING, 8, tile), f32),
            pltpu.VMEM((RING, 2 * RING, tile), f32),
            pltpu.VMEM((RING, 2 * RING, tile), f32),
            pltpu.VMEM((RING, hd, rows), bf16),
            pltpu.VMEM((far, hd, rows), bf16),
            pltpu.VMEM((far, codes, hd), bf16),
            pltpu.VMEM((far, codes, hd), bf16),
            pltpu.VMEM((RING, 8, codes), f32),
            pltpu.VMEM((far, 8, codes), f32),
            dma((4 * RING,)),
            dma,
            dma,
            dma((2,)),
            dma((far,)), dma((far,)),
            dma((max(heads - 1, 1),)), dma((max(heads - 1, 1),)),
            dma((2, far)), dma((2, far)),
            dma((RING, far)), dma((RING, far)),
            dma((far,)), dma((far,)),
            dma((max(heads - 1, 1),)), dma((max(heads - 1, 1),)),
            dma((far, 2)), dma((far, 2)),
            dma((far, 2)), dma((far, 2)),
        ],
        compiler_params=pltpu.CompilerParams(
            collective_id=0, has_side_effects=True, vmem_limit_bytes=63 * 2**20
        ),
    )(tokens, codebook, ema_counts, ema_sums)
    return pl.pallas_call(
        place,
        out_shape=(
            jax.ShapeDtypeStruct(tokens.shape, bf16),
            jax.ShapeDtypeStruct(ema_counts.shape, f32),
            jax.ShapeDtypeStruct(ema_sums.shape, f32),
        ),
        in_specs=[vmem] * 3,
        out_specs=(vmem,) * 3,
    )(pieces, counts, book)


def solution(mesh):
    placed = (
        P(("head", "code"), None),
        P("head", "code", None),
        P("head", "code"),
        P("head", "code", None),
    )
    return jax.shard_map(
        shards,
        mesh=mesh,
        in_specs=placed,
        out_specs=(P(("head", "code"), None), P("head", "code"), P("head", "code", None)),
        check_vma=False,
    )
```

```python
import functools

import jax
import jax.numpy as jnp
from jax import lax
from jax.experimental import pallas as pl
from jax.experimental.pallas import tpu as pltpu
from jax.sharding import PartitionSpec as P

MESH = pl.DeviceIdType.MESH
bf16 = jnp.bfloat16
f32 = jnp.float32
momentum = 0.8
half_log2e = 0.5 * 1.4426950408889634
RING = 4
QROWS = 144


def dot(a, b, ca, cb):
    return lax.dot_general(a, b, (((ca,), (cb,)), ((), ())), preferred_element_type=f32)


def gray(s):
    return s + (s // 2) * (1 - 2 * (s % 2))


def kernel(
    heads, tok_ref, cb_ref, cnt_ref, sums_hbm,
    oland, ncnt_ref, ncb_hbm, spill,
    e_buf, s_buf, m_buf, c_land, naug, c_t, naug_next, c_t_next, tsend, x_land, q_acc, stat, stat_land, mloc, f_buf,
    qsend, qland, nsend, nland, ksend, kland,
    e_sem, sums_sem, own_sem, book_sem, c_ss, c_rs, h_ss, h_rs, y_ss, y_rs, st_ss, st_rs, q_ss, q_rs, o_ss, o_rs, n_ss, n_rs, k_ss, k_rs,
):
    h = lax.axis_index("head")
    code = lax.axis_index("code")
    core = lax.rem(h, 2)
    first, second = code // RING, code % RING
    y = first * (1 - core) + second * core
    z = second * (1 - core) + first * core
    y_step, z_step = RING - (RING - 1) * core, 1 + (RING - 1) * core
    width = tok_ref.shape[0]
    codes, hd = cb_ref.shape[1], cb_ref.shape[2]
    tile = x_land.shape[2] // 2

    def at_head(d):
        return (lax.rem(h + d, heads), code)

    def at_y(d):
        return (h, lax.rem(y + d, RING) * y_step + z * z_step)

    def at_z(d):
        return (h, y * y_step + lax.rem(z + d, RING) * z_step)

    def remote(src, dst, ss, rs, where):
        return pltpu.make_async_remote_copy(
            src_ref=src, dst_ref=dst, send_sem=ss, recv_sem=rs, device_id=where, device_id_type=MESH
        )

    sums_buf = s_buf.at[1, :, pl.ds(0, hd)]

    def sum_copy():
        return pltpu.make_async_copy(sums_hbm.at[0], sums_buf, sums_sem)

    barrier = pltpu.get_barrier_semaphore()
    for d in range(1, heads):
        pl.semaphore_signal(barrier, inc=1, device_id=at_head(d), device_id_type=MESH)
    for d in range(1, RING):
        pl.semaphore_signal(barrier, inc=1, device_id=at_y(d), device_id_type=MESH)
        pl.semaphore_signal(barrier, inc=1, device_id=at_z(d), device_id_type=MESH)
    for g in range(heads):
        block = tok_ref[:, g * hd:(g + 1) * hd].astype(f32)
        tsend[g] = jnp.transpose(block).astype(bf16)
    pl.semaphore_wait(barrier, heads - 1 + 2 * (RING - 1))

    def head_copy(d):
        other = lax.rem(h + d, 2)
        block = first * (1 - other) + second * other
        return remote(
            tsend.at[lax.rem(h + d, heads)],
            x_land.at[block, :, pl.ds(pl.multiple_of(h * width, 128), width)],
            h_ss.at[d - 1], h_rs.at[d - 1], at_head(d),
        )

    def c_copy(d):
        return remote(cb_ref.at[0], c_land.at[z], c_ss.at[d - 1], c_rs.at[d - 1], at_z(d))

    def y_copy(d, half):
        block = x_land.at[y, :, pl.ds(half * tile, tile)]
        return remote(block, block, y_ss.at[half, d - 1], y_rs.at[half, d - 1], at_y(d))

    for d in range(1, heads):
        head_copy(d).start()
    for d in (1, 3):
        c_copy(d).start()
    x_land[y, :, pl.ds(pl.multiple_of(h * width, 128), width)] = tsend[h]
    c_land[z] = cb_ref[0]

    tail = lax.broadcasted_iota(jnp.int32, (QROWS - hd, codes), 0)
    for slot in range(2):
        c_t[slot, hd:, :] = jnp.where(tail == 0, 1.0, 0.0).astype(bf16)
    row = lax.broadcasted_iota(jnp.int32, (hd, tile), 0)
    ones_rows = jnp.where(row < 3, 1.0, 0.0).astype(bf16)

    def prepare(aug, cols, zb, start, count):
        part = pl.ds(start, count)
        c = c_land[zb, part, :].astype(f32)
        n = -0.5 * jnp.sum(c * c, axis=1, keepdims=True)
        hi = n.astype(bf16).astype(f32)
        rest = n - hi
        mid = rest.astype(bf16).astype(f32)
        low = rest - mid
        lane = lax.broadcasted_iota(jnp.int32, (count, hd), 1)
        aug[part, :] = jnp.where(lane == 0, hi, jnp.where(lane == 1, mid, jnp.where(lane == 2, low, 0.0))).astype(bf16)
        cols[0:hd, part] = jnp.transpose(c).astype(bf16)

    prepare(naug.at[0], c_t.at[0], z, 0, codes)
    stat[...] = jnp.full(stat.shape, -3e38, f32)
    q_acc[...] = jnp.zeros(q_acc.shape, f32)

    for d in range(1, heads):
        head_copy(d).wait()
    for half in range(2):
        for d in (1, 3):
            y_copy(d, half).start()

    def row_block(j, s):
        first = 1 - (j + 3) // 4
        return lax.rem(first * (y + gray(s)) + (1 - first) * s, RING)

    def logits(j, s, half, slot):
        zb = lax.rem(z + gray(j), RING)
        yb = row_block(j, s)
        left = jnp.concatenate([c_land[zb], naug[j % 2]], axis=1)
        right = jnp.concatenate([x_land[yb, :, half * tile:(half + 1) * tile], ones_rows], axis=0)
        out = dot(left, right, 1, 0)
        s_buf[slot] = out
        m_buf[slot] = jnp.max(out, axis=0, keepdims=True)

    def finish(j, s, half, slot):
        yb = row_block(j, s)
        es = (j % 2) * (2 * RING) + 2 * s + half
        m = m_buf[slot]
        e = jnp.exp2((s_buf[slot] - m) * half_log2e).astype(bf16)
        e_buf[es] = e
        q = dot(c_t[j % 2], e, 1, 0)
        m_old = stat[yb, half:half + 1, :]
        m_new = jnp.maximum(m_old, m)
        q = q_acc[2 * yb + half] * jnp.exp2((m_old - m_new) * half_log2e) + q * jnp.exp2((m - m_new) * half_log2e)
        q_acc[2 * yb + half] = q
        stat[yb, half:half + 1, :] = m_new
        stat[yb, 2 + half:3 + half, :] = q[hd:hd + 1, :]
        mloc[yb, pl.ds(2 * j + half, 1), :] = m

    def spill_copy(es):
        return pltpu.make_async_copy(e_buf.at[es], spill.at[es], e_sem.at[es])

    def fetch_copy(es):
        return pltpu.make_async_copy(spill.at[es], e_buf.at[es], e_sem.at[es])

    def wait_rows(s, half):
        o = gray(s)
        block = x_land.at[lax.rem(y + o, RING), :, pl.ds(half * tile, tile)]
        remote(block, block, y_ss.at[half, 3 - o], y_rs.at[half, 3 - o], at_y(4 - o)).wait_recv()

    def wait_codes(j):
        o = gray(j)
        remote(
            cb_ref.at[0], c_land.at[lax.rem(z + o, RING)], c_ss.at[3 - o], c_rs.at[3 - o], at_z(4 - o)
        ).wait_recv()

    def stat_copy(b, d):
        return remote(stat.at[b], stat_land.at[d - 1, b], st_ss.at[b, d - 1], st_rs.at[b, d - 1], at_y(d))

    pairs = RING * RING
    quarter = codes // RING
    logits(0, 0, 0, 0)

    def first_step(p, _):
        @pl.when(p > 0)
        def _():
            wait_rows(p, 1)

        @pl.when(p == 1)
        def _():
            for half in range(2):
                for d in (1, 3):
                    y_copy(d, half).wait_send()
            for half in range(2):
                y_copy(2, half).start()

        @pl.when(p == 2)
        def _():
            for d in (1, 3):
                c_copy(d).wait_send()
            c_copy(2).start()

        logits(0, p, 1, 1)
        finish(0, p, 0, 0)

        @pl.when(p < RING - 1)
        def _():
            wait_rows(p + 1, 0)

        @pl.when(p == RING - 1)
        def _():
            wait_codes(1)
            prepare(naug.at[1], c_t.at[1], lax.rem(z + 1, RING), 0, codes)

        logits((p + 1) // RING, (p + 1) % RING, 0, 0)
        finish(0, p, 1, 1)
        spill_copy(2 * p).start()
        spill_copy(2 * p + 1).start()
        return 0

    def step(p, _):
        j, s = p // RING, p % RING
        pn = (p + 1) % pairs
        jn, sn = pn // RING, pn % RING
        es = (j % 2) * (2 * RING) + 2 * s

        @pl.when((s == 0) & (j < RING - 1))
        def _():
            wait_codes(j + 1)

        ahead = lax.rem(z + gray((j + 1) % RING), RING)

        @pl.when((s == RING - 1) & (j < RING - 1))
        def _():
            slot = (j + 1) % 2
            done = (RING - 1) * quarter
            naug[slot, 0:done, :] = naug_next[0:done, :]
            c_t[slot, 0:hd, 0:done] = c_t_next[0:hd, 0:done]
            prepare(naug.at[slot], c_t.at[slot], ahead, done, quarter)

        @pl.when(j >= 2)
        def _():
            spill_copy(es).wait()
            spill_copy(es + 1).wait()

        logits(j, s, 1, 1)
        finish(j, s, 0, 0)
        logits(jn, sn, 0, 0)
        finish(j, s, 1, 1)
        prepare(naug_next, c_t_next, ahead, pl.multiple_of(s * quarter, quarter), quarter)

        @pl.when(j == RING - 1)
        def _():
            for d in range(1, RING):
                stat_copy(s, d).start()

        @pl.when(j < 2)
        def _():
            spill_copy(es).start()
            spill_copy(es + 1).start()

        return 0

    lax.fori_loop(0, RING, first_step, 0)
    lax.fori_loop(RING, pairs, step, 0)
    sum_copy().start()

    def q_copy(b):
        d = lax.rem(b - y + RING, RING)
        return remote(qsend.at[b], qland.at[d - 1], q_ss.at[d - 1], q_rs.at[d - 1], (h, b * y_step + z * z_step))

    def q_wait(d):
        b = lax.rem(y + d, RING)
        return remote(qsend.at[b], qland.at[d - 1], q_ss.at[d - 1], q_rs.at[d - 1], (h, b * y_step + z * z_step))

    def totals(b):
        for d in range(1, RING):
            stat_copy(b, d).wait()
        m, l = stat[b, 0:2, :], stat[b, 2:4, :]
        top = m
        for d in range(1, RING):
            top = jnp.maximum(top, stat_land[d - 1, b, 0:2, :])
        total = l * jnp.exp2((m - top) * half_log2e)
        for d in range(1, RING):
            total = total + stat_land[d - 1, b, 2:4, :] * jnp.exp2((stat_land[d - 1, b, 0:2, :] - top) * half_log2e)
        inverse = 1.0 / total
        gain = jnp.exp2((m - top) * half_log2e) * inverse
        even = lax.broadcasted_iota(jnp.int32, (2 * RING, tile), 0) % 2 == 0
        top_all = jnp.where(even, top[0:1, :], top[1:2, :])
        f_buf[b] = jnp.exp2((mloc[b] - top_all) * half_log2e) * jnp.where(even, inverse[0:1, :], inverse[1:2, :])
        for half in range(2):
            cols = slice(half * tile, (half + 1) * tile)
            qsend[b, :, cols] = (q_acc[2 * b + half, 0:hd, :] * gain[half:half + 1, :]).astype(bf16)

        @pl.when(y != b)
        def _():
            q_copy(b).start()

    def o_copy(d):
        return remote(tsend.at[lax.rem(h + d, heads)], oland.at[h], o_ss.at[d - 1], o_rs.at[d - 1], at_head(d))

    def send_quantized():
        for d in range(1, RING):
            q_wait(d).wait()
        for g in range(heads):
            cols = slice(g * width, (g + 1) * width)
            block = qsend[y, :, cols].astype(f32)
            for d in range(1, RING):
                block = block + qland[d - 1, :, cols].astype(f32)
            tsend[g] = jnp.transpose(block).astype(bf16)
        for d in range(1, heads):
            o_copy(d).start()
        pltpu.make_async_copy(tsend.at[h], oland.at[h], own_sem).start()

    group = 4
    half_codes = codes // 2
    acc = s_buf.at[0, :, pl.ds(0, 2 * hd)]
    pad_row = lax.broadcasted_iota(jnp.int32, (hd, tile), 0)

    def n_copy(jj, d, ch):
        part = pl.ds(pl.multiple_of(ch * half_codes, half_codes), half_codes)
        return remote(nsend.at[jj, part], nland.at[d - 1, part], n_ss.at[d - 1, ch], n_rs.at[d - 1, ch], at_z(d))

    def k_copy(jj, d, ch):
        part = pl.ds(pl.multiple_of(ch * half_codes, half_codes), half_codes)
        return remote(
            ksend.at[jj, :, part], kland.at[d - 1, :, part], k_ss.at[d - 1, ch], k_rs.at[d - 1, ch], at_z(d)
        )

    def scaled(j, t):
        yb = row_block(j, t // 2)
        f = f_buf[yb, 2 * j + t % 2:2 * j + t % 2 + 1, :]
        x = x_land[yb, :, (t % 2) * tile:(t % 2 + 1) * tile].astype(f32)
        f_hi = f.astype(bf16).astype(f32)
        extra = jnp.where(pad_row == 0, f_hi, jnp.where(pad_row == 1, f - f_hi, 0.0))
        return jnp.concatenate([(x * f).astype(bf16), extra.astype(bf16)], axis=0)

    routes = (2, 3, 1)
    for jj in range(RING):
        j = RING - 1 - jj
        base = (j % 2) * (2 * RING)
        for g in range(2 * RING // group):
            tiles = range(g * group, (g + 1) * group)
            if jj == 0:
                for b in range(g * group // 2, (g + 1) * group // 2):
                    totals(b)
            if jj >= 2:
                for t in tiles:
                    fetch_copy(base + t).wait()

            def some_codes(ch, _, j=j, jj=jj, base=base, tiles=tiles, g=g):
                part = pl.ds(pl.multiple_of(ch * half_codes, half_codes), half_codes)
                left = jnp.concatenate([e_buf[base + t, part, :] for t in tiles], axis=1)
                right = jnp.concatenate([scaled(j, t) for t in tiles], axis=1)
                out = dot(left, right, 1, 1)
                if g > 0:
                    out = out + acc[part, :]
                if g < 2 * RING // group - 1:
                    acc[part, :] = out
                else:
                    columns = jnp.transpose(out[:, hd:2 * hd])
                    row = columns[0:1, :] + columns[1:2, :]
                    ksend[jj, :, part] = row
                    if j > 0:
                        nsend[jj, part, :] = out[:, 0:hd].astype(bf16)
                        n_copy(jj, routes[jj], ch).start()
                        k_copy(jj, routes[jj], ch).start()
                    else:
                        acc[part, 0:hd] = out[:, 0:hd]
                return 0

            lax.fori_loop(0, 2, some_codes, 0)
            if jj < 2:
                for t in tiles:
                    fetch_copy(base + t).start()
        if jj == 2:
            send_quantized()

    sum_copy().wait()
    book_copies = []
    for ch in range(2):
        part = slice(ch * half_codes, (ch + 1) * half_codes)
        for jj, d in enumerate(routes):
            n_copy(jj, d, ch).wait()
            k_copy(jj, d, ch).wait()
        row = ksend[RING - 1, :, part]
        numerators = acc[part, 0:hd]
        for d in range(1, RING):
            row = row + kland[d - 1, :, part]
            numerators = numerators + nland[d - 1, part, :].astype(f32)
        new_counts = momentum * cnt_ref[:, part] + (1.0 - momentum) * row
        ncnt_ref[:, part] = new_counts
        inverse_counts = jnp.transpose(jnp.broadcast_to(1.0 / new_counts, (8, half_codes)))[:, 0:1]
        sums_buf[part, :] = (momentum * sums_buf[part, :] + (1.0 - momentum) * numerators) * inverse_counts
        book_copies.append(
            pltpu.make_async_copy(
                sums_buf.at[pl.ds(ch * half_codes, half_codes)],
                ncb_hbm.at[0, pl.ds(ch * half_codes, half_codes)],
                book_sem.at[ch],
            )
        )
        book_copies[-1].start()
    for d in range(1, heads):
        o_copy(d).wait()
    pltpu.make_async_copy(tsend.at[h], oland.at[h], own_sem).wait()
    c_copy(2).wait_send()
    for half in range(2):
        y_copy(2, half).wait_send()
    for copy in book_copies:
        copy.wait()


def place(oland, counts, book, quant_ref, ncnt_ref, ncb_ref):
    heads, _, hd = oland.shape
    for g in range(heads):
        quant_ref[:, g * hd:(g + 1) * hd] = oland[g]
    ncnt_ref[...] = counts[...]
    ncb_ref[...] = book[...]


def shards(tokens, codebook, ema_counts, ema_sums):
    heads = lax.axis_size("head")
    width, _ = tokens.shape
    _, codes, hd = codebook.shape
    rows = heads * width
    tile = rows // 2
    vmem = pl.BlockSpec(memory_space=pltpu.VMEM)
    dma = pltpu.SemaphoreType.DMA
    anywhere = pl.BlockSpec(memory_space=pl.ANY)
    far = RING - 1
    pieces, counts, book, _ = pl.pallas_call(
        functools.partial(kernel, heads),
        out_shape=(
            jax.ShapeDtypeStruct((heads, width, hd), bf16),
            jax.ShapeDtypeStruct(ema_counts.shape, f32),
            jax.ShapeDtypeStruct(ema_sums.shape, f32),
            jax.ShapeDtypeStruct((4 * RING, codes, tile), bf16),
        ),
        in_specs=[vmem, vmem, vmem, anywhere],
        out_specs=(anywhere, vmem, anywhere, anywhere),
        scratch_shapes=[
            pltpu.VMEM((4 * RING, codes, tile), bf16),
            pltpu.VMEM((2, codes, tile), f32),
            pltpu.VMEM((2, 1, tile), f32),
            pltpu.VMEM((RING, codes, hd), bf16),
            pltpu.VMEM((2, codes, hd), bf16),
            pltpu.VMEM((2, QROWS, codes), bf16),
            pltpu.VMEM((codes, hd), bf16),
            pltpu.VMEM((hd, codes), bf16),
            pltpu.VMEM((heads, hd, width), bf16),
            pltpu.VMEM((RING, hd, rows), bf16),
            pltpu.VMEM((2 * RING, QROWS, tile), f32),
            pltpu.VMEM((RING, 8, tile), f32),
            pltpu.VMEM((far, RING, 8, tile), f32),
            pltpu.VMEM((RING, 2 * RING, tile), f32),
            pltpu.VMEM((RING, 2 * RING, tile), f32),
            pltpu.VMEM((RING, hd, rows), bf16),
            pltpu.VMEM((far, hd, rows), bf16),
            pltpu.VMEM((far, codes, hd), bf16),
            pltpu.VMEM((far, codes, hd), bf16),
            pltpu.VMEM((RING, 1, codes), f32),
            pltpu.VMEM((far, 1, codes), f32),
            dma((4 * RING,)),
            dma,
            dma,
            dma((2,)),
            dma((far,)), dma((far,)),
            dma((max(heads - 1, 1),)), dma((max(heads - 1, 1),)),
            dma((2, far)), dma((2, far)),
            dma((RING, far)), dma((RING, far)),
            dma((far,)), dma((far,)),
            dma((max(heads - 1, 1),)), dma((max(heads - 1, 1),)),
            dma((far, 2)), dma((far, 2)),
            dma((far, 2)), dma((far, 2)),
        ],
        compiler_params=pltpu.CompilerParams(
            collective_id=0, has_side_effects=True, vmem_limit_bytes=63 * 2**20
        ),
    )(tokens, codebook, ema_counts, ema_sums)
    return pl.pallas_call(
        place,
        out_shape=(
            jax.ShapeDtypeStruct(tokens.shape, bf16),
            jax.ShapeDtypeStruct(ema_counts.shape, f32),
            jax.ShapeDtypeStruct(ema_sums.shape, f32),
        ),
        in_specs=[vmem] * 3,
        out_specs=(vmem,) * 3,
    )(pieces, counts, book)


def solution(mesh):
    placed = (
        P(("head", "code"), None),
        P("head", "code", None),
        P("head", "code"),
        P("head", "code", None),
    )
    return jax.shard_map(
        shards,
        mesh=mesh,
        in_specs=placed,
        out_specs=(P(("head", "code"), None), P("head", "code"), P("head", "code", None)),
        check_vma=False,
    )
```

```python
import functools

import jax
import jax.numpy as jnp
from jax import lax
from jax.experimental import pallas as pl
from jax.experimental.pallas import tpu as pltpu
from jax.sharding import PartitionSpec as P

MESH = pl.DeviceIdType.MESH
bf16 = jnp.bfloat16
f32 = jnp.float32
momentum = 0.8
half_log2e = 0.5 * 1.4426950408889634
RING = 4
QROWS = 144


def dot(a, b, ca, cb):
    return lax.dot_general(a, b, (((ca,), (cb,)), ((), ())), preferred_element_type=f32)


def gray(s):
    return s + (s // 2) * (1 - 2 * (s % 2))


def kernel(
    heads, tok_hbm, cb_hbm, cnt_ref, sums_hbm,
    oland, ncnt_ref, ncb_hbm, spill,
    e_buf, s_buf, m_buf, c_land, naug, c_t, naug_next, c_t_next, tok_ref, tsend, x_land, q_acc, stat, stat_land, mloc, f_buf, gain,
    qsend, qland, nsend, nland, ksend, kland,
    e_sem, sums_sem, own_sem, book_sem, in_sem, c_ss, c_rs, h_ss, h_rs, y_ss, y_rs, st_ss, st_rs, q_ss, q_rs, o_ss, o_rs, n_ss, n_rs, k_ss, k_rs,
):
    h = lax.axis_index("head")
    code = lax.axis_index("code")
    core = lax.rem(h, 2)
    first, second = code // RING, code % RING
    y = first * (1 - core) + second * core
    z = second * (1 - core) + first * core
    y_step, z_step = RING - (RING - 1) * core, 1 + (RING - 1) * core
    width = tok_ref.shape[0]
    codes, hd = cb_hbm.shape[1], cb_hbm.shape[2]
    tile = x_land.shape[2] // 2

    def at_head(d):
        return (lax.rem(h + d, heads), code)

    def at_y(d):
        return (h, lax.rem(y + d, RING) * y_step + z * z_step)

    def at_z(d):
        return (h, y * y_step + lax.rem(z + d, RING) * z_step)

    def remote(src, dst, ss, rs, where):
        return pltpu.make_async_remote_copy(
            src_ref=src, dst_ref=dst, send_sem=ss, recv_sem=rs, device_id=where, device_id_type=MESH
        )

    sums_buf = s_buf.at[1, :, pl.ds(0, hd)]

    def sum_copy():
        return pltpu.make_async_copy(sums_hbm.at[0], sums_buf, sums_sem)

    tok_copy = pltpu.make_async_copy(tok_hbm, tok_ref, in_sem.at[0])
    tok_copy.start()
    own_codes = pltpu.make_async_copy(cb_hbm.at[0], c_land.at[z], in_sem.at[1])
    own_codes.start()

    barrier = pltpu.get_barrier_semaphore()
    for d in range(1, heads):
        pl.semaphore_signal(barrier, inc=1, device_id=at_head(d), device_id_type=MESH)
    for d in range(1, RING):
        pl.semaphore_signal(barrier, inc=1, device_id=at_y(d), device_id_type=MESH)
        pl.semaphore_signal(barrier, inc=1, device_id=at_z(d), device_id_type=MESH)
    tok_copy.wait()
    for g in range(heads):
        block = tok_ref[:, g * hd:(g + 1) * hd].astype(f32)
        tsend[g] = jnp.transpose(block).astype(bf16)
    pl.semaphore_wait(barrier, heads - 1 + 2 * (RING - 1))

    def head_copy(d):
        other = lax.rem(h + d, 2)
        block = first * (1 - other) + second * other
        return remote(
            tsend.at[lax.rem(h + d, heads)],
            x_land.at[block, :, pl.ds(pl.multiple_of(h * width, 128), width)],
            h_ss.at[d - 1], h_rs.at[d - 1], at_head(d),
        )

    def c_copy(d):
        return remote(cb_hbm.at[0], c_land.at[z], c_ss.at[d - 1], c_rs.at[d - 1], at_z(d))

    def y_copy(d, half):
        block = x_land.at[y, :, pl.ds(half * tile, tile)]
        return remote(block, block, y_ss.at[half, d - 1], y_rs.at[half, d - 1], at_y(d))

    for d in range(1, heads):
        head_copy(d).start()
    for d in (1, 3):
        c_copy(d).start()
    x_land[y, :, pl.ds(pl.multiple_of(h * width, 128), width)] = tsend[h]

    tail = lax.broadcasted_iota(jnp.int32, (QROWS - hd, codes), 0)
    for slot in range(2):
        c_t[slot, hd:, :] = jnp.where(tail == 0, 1.0, 0.0).astype(bf16)
    row = lax.broadcasted_iota(jnp.int32, (hd, tile), 0)
    ones_rows = jnp.where(row < 3, 1.0, 0.0).astype(bf16)

    def prepare(aug, cols, zb, start, count):
        part = pl.ds(start, count)
        c = c_land[zb, part, :].astype(f32)
        n = -0.5 * jnp.sum(c * c, axis=1, keepdims=True)
        hi = n.astype(bf16).astype(f32)
        rest = n - hi
        mid = rest.astype(bf16).astype(f32)
        low = rest - mid
        lane = lax.broadcasted_iota(jnp.int32, (count, hd), 1)
        aug[part, :] = jnp.where(lane == 0, hi, jnp.where(lane == 1, mid, jnp.where(lane == 2, low, 0.0))).astype(bf16)
        cols[0:hd, part] = jnp.transpose(c).astype(bf16)

    own_codes.wait()
    prepare(naug.at[0], c_t.at[0], z, 0, codes)
    stat[...] = jnp.full(stat.shape, -3e38, f32)
    q_acc[...] = jnp.zeros(q_acc.shape, f32)

    for d in range(1, heads):
        head_copy(d).wait()
    for half in range(2):
        for d in (1, 3):
            y_copy(d, half).start()

    def row_block(j, s):
        first = 1 - (j + 3) // 4
        return lax.rem(first * (y + gray(s)) + (1 - first) * s, RING)

    def logits(j, s, half, slot):
        zb = lax.rem(z + gray(j), RING)
        yb = row_block(j, s)
        left = jnp.concatenate([c_land[zb], naug[j % 2]], axis=1)
        right = jnp.concatenate([x_land[yb, :, half * tile:(half + 1) * tile], ones_rows], axis=0)
        out = dot(left, right, 1, 0)
        s_buf[slot] = out
        m_buf[slot] = jnp.max(out, axis=0, keepdims=True)

    def finish(j, s, half, slot):
        yb = row_block(j, s)
        es = (j % 2) * (2 * RING) + 2 * s + half
        m = m_buf[slot]
        e = jnp.exp2((s_buf[slot] - m) * half_log2e).astype(bf16)
        e_buf[es] = e
        q = dot(c_t[j % 2], e, 1, 0)
        m_old = stat[yb, half:half + 1, :]
        m_new = jnp.maximum(m_old, m)
        q = q_acc[2 * yb + half] * jnp.exp2((m_old - m_new) * half_log2e) + q * jnp.exp2((m - m_new) * half_log2e)
        q_acc[2 * yb + half] = q
        stat[yb, half:half + 1, :] = m_new
        stat[yb, 2 + half:3 + half, :] = q[hd:hd + 1, :]
        mloc[yb, pl.ds(2 * j + half, 1), :] = m

    def spill_copy(es):
        return pltpu.make_async_copy(e_buf.at[es], spill.at[es], e_sem.at[es])

    def fetch_copy(es):
        return pltpu.make_async_copy(spill.at[es], e_buf.at[es], e_sem.at[es])

    def wait_rows(s, half):
        o = gray(s)
        block = x_land.at[lax.rem(y + o, RING), :, pl.ds(half * tile, tile)]
        remote(block, block, y_ss.at[half, 3 - o], y_rs.at[half, 3 - o], at_y(4 - o)).wait_recv()

    def wait_codes(j):
        o = gray(j)
        remote(
            cb_hbm.at[0], c_land.at[lax.rem(z + o, RING)], c_ss.at[3 - o], c_rs.at[3 - o], at_z(4 - o)
        ).wait_recv()

    def stat_copy(b, d):
        return remote(stat.at[b], stat_land.at[d - 1, b], st_ss.at[b, d - 1], st_rs.at[b, d - 1], at_y(d))

    pairs = RING * RING
    quarter = codes // RING
    logits(0, 0, 0, 0)

    def first_step(p, late):
        @pl.when(p > 0)
        def _():
            wait_rows(p, 1)

        if late:
            @pl.when(p == 2)
            def _():
                for d in (1, 3):
                    c_copy(d).wait_send()
                c_copy(2).start()
                wait_codes(1)
        else:
            @pl.when(p == 1)
            def _():
                for half in range(2):
                    for d in (1, 3):
                        y_copy(d, half).wait_send()
                for half in range(2):
                    y_copy(2, half).start()

        logits(0, p, 1, 1)
        finish(0, p, 0, 0)
        if late:
            start = pl.multiple_of((p - 2) * (codes // 2), codes // 2)
            prepare(naug.at[1], c_t.at[1], lax.rem(z + 1, RING), start, codes // 2)

        @pl.when(p < RING - 1)
        def _():
            wait_rows(p + 1, 0)

        logits((p + 1) // RING, (p + 1) % RING, 0, 0)
        finish(0, p, 1, 1)
        spill_copy(2 * p).start()
        spill_copy(2 * p + 1).start()
        return 0

    def step(p, _):
        j, s = p // RING, p % RING
        pn = (p + 1) % pairs
        jn, sn = pn // RING, pn % RING
        es = (j % 2) * (2 * RING) + 2 * s

        @pl.when((s == 0) & (j < RING - 1))
        def _():
            wait_codes(j + 1)

        ahead = lax.rem(z + gray((j + 1) % RING), RING)

        @pl.when((s == RING - 1) & (j < RING - 1))
        def _():
            slot = (j + 1) % 2
            done = (RING - 1) * quarter
            naug[slot, 0:done, :] = naug_next[0:done, :]
            c_t[slot, 0:hd, 0:done] = c_t_next[0:hd, 0:done]
            prepare(naug.at[slot], c_t.at[slot], ahead, done, quarter)

        @pl.when(j >= 2)
        def _():
            spill_copy(es).wait()
            spill_copy(es + 1).wait()

        logits(j, s, 1, 1)
        finish(j, s, 0, 0)
        logits(jn, sn, 0, 0)
        finish(j, s, 1, 1)
        prepare(naug_next, c_t_next, ahead, pl.multiple_of(s * quarter, quarter), quarter)

        @pl.when(j == RING - 1)
        def _():
            for d in range(1, RING):
                stat_copy(s, d).start()

        @pl.when(j < 2)
        def _():
            spill_copy(es).start()
            spill_copy(es + 1).start()

        return 0

    lax.fori_loop(0, 2, lambda p, _: first_step(p, False), 0)
    lax.fori_loop(2, RING, lambda p, _: first_step(p, True), 0)
    lax.fori_loop(RING, pairs, step, 0)
    sum_copy().start()

    def q_copy(b):
        d = lax.rem(b - y + RING, RING)
        return remote(qsend.at[b], qland.at[d - 1], q_ss.at[d - 1], q_rs.at[d - 1], (h, b * y_step + z * z_step))

    def q_wait(d):
        b = lax.rem(y + d, RING)
        return remote(qsend.at[b], qland.at[d - 1], q_ss.at[d - 1], q_rs.at[d - 1], (h, b * y_step + z * z_step))

    def totals(b):
        for d in range(1, RING):
            stat_copy(b, d).wait()
        m, l = stat[b, 0:2, :], stat[b, 2:4, :]
        top = m
        for d in range(1, RING):
            top = jnp.maximum(top, stat_land[d - 1, b, 0:2, :])
        total = l * jnp.exp2((m - top) * half_log2e)
        for d in range(1, RING):
            total = total + stat_land[d - 1, b, 2:4, :] * jnp.exp2((stat_land[d - 1, b, 0:2, :] - top) * half_log2e)
        inverse = 1.0 / total
        gain[b, 0:2, :] = jnp.exp2((m - top) * half_log2e) * inverse
        even = lax.broadcasted_iota(jnp.int32, (2 * RING, tile), 0) % 2 == 0
        top_all = jnp.where(even, top[0:1, :], top[1:2, :])
        f_buf[b] = jnp.exp2((mloc[b] - top_all) * half_log2e) * jnp.where(even, inverse[0:1, :], inverse[1:2, :])

    def quantized_rows(b):
        for half in range(2):
            cols = slice(half * tile, (half + 1) * tile)
            qsend[b, :, cols] = (q_acc[2 * b + half, 0:hd, :] * gain[b, half:half + 1, :]).astype(bf16)

    def send_rows(b):
        @pl.when(y != b)
        def _():
            q_copy(b).start()

    def o_copy(d):
        return remote(tsend.at[lax.rem(h + d, heads)], oland.at[h], o_ss.at[d - 1], o_rs.at[d - 1], at_head(d))

    def quantized_part(part):
        for g in range(heads // 2):
            head = (heads // 2) * part + g
            cols = pl.ds(pl.multiple_of(head * width, 128), width)
            block = qsend[y, :, cols].astype(f32)
            for d in range(1, RING):
                block = block + qland[d - 1, :, cols].astype(f32)
            tsend[head] = jnp.transpose(block).astype(bf16)

    def send_quantized():
        for d in range(1, heads):
            o_copy(d).start()
        pltpu.make_async_copy(tsend.at[h], oland.at[h], own_sem).start()

    group = 4
    half_codes = codes // 2
    acc = s_buf.at[0, :, pl.ds(0, 2 * hd)]
    pad_row = lax.broadcasted_iota(jnp.int32, (hd, tile), 0)

    def n_copy(jj, d, ch):
        part = pl.ds(pl.multiple_of(ch * half_codes, half_codes), half_codes)
        return remote(nsend.at[jj, part], nland.at[d - 1, part], n_ss.at[d - 1, ch], n_rs.at[d - 1, ch], at_z(d))

    def k_copy(jj, d, ch):
        part = pl.ds(pl.multiple_of(ch * half_codes, half_codes), half_codes)
        return remote(
            ksend.at[jj, :, part], kland.at[d - 1, :, part], k_ss.at[d - 1, ch], k_rs.at[d - 1, ch], at_z(d)
        )

    def scaled(j, t):
        yb = row_block(j, t // 2)
        f = f_buf[yb, 2 * j + t % 2:2 * j + t % 2 + 1, :]
        x = x_land[yb, :, (t % 2) * tile:(t % 2 + 1) * tile].astype(f32)
        f_hi = f.astype(bf16).astype(f32)
        extra = jnp.where(pad_row == 0, f_hi, jnp.where(pad_row == 1, f - f_hi, 0.0))
        return jnp.concatenate([(x * f).astype(bf16), extra.astype(bf16)], axis=0)

    routes = (2, 3, 1)
    for jj in range(RING):
        j = RING - 1 - jj
        base = (j % 2) * (2 * RING)
        for g in range(2 * RING // group):
            tiles = range(g * group, (g + 1) * group)
            if jj == 0:
                for b in range(g * group // 2, (g + 1) * group // 2):
                    totals(b)
            if jj >= 2:
                for t in tiles:
                    fetch_copy(base + t).wait()
            if j == 0 and g == 0:
                for d in range(1, RING):
                    q_wait(d).wait()

            def some_codes(ch, _, j=j, jj=jj, base=base, tiles=tiles, g=g):
                part = pl.ds(pl.multiple_of(ch * half_codes, half_codes), half_codes)
                left = jnp.concatenate([e_buf[base + t, part, :] for t in tiles], axis=1)
                right = jnp.concatenate([scaled(j, t) for t in tiles], axis=1)
                out = dot(left, right, 1, 1)
                if jj == 0:
                    quantized_rows(2 * g + ch)
                if j == 0 and g == 0:
                    quantized_part(ch)
                if g > 0:
                    out = out + acc[part, :]
                if g < 2 * RING // group - 1:
                    acc[part, :] = out
                else:
                    columns = jnp.transpose(out[:, hd:2 * hd])
                    row = columns[0:1, :] + columns[1:2, :]
                    ksend[jj, :, part] = row
                    if j > 0:
                        nsend[jj, part, :] = out[:, 0:hd].astype(bf16)
                        n_copy(jj, routes[jj], ch).start()
                        k_copy(jj, routes[jj], ch).start()
                    else:
                        acc[part, 0:hd] = out[:, 0:hd]
                if jj == 0:
                    send_rows(2 * g + ch)
                return 0

            lax.fori_loop(0, 2, some_codes, 0)
            if jj < 2:
                for t in tiles:
                    fetch_copy(base + t).start()
            if j == 0 and g == 0:
                send_quantized()

    sum_copy().wait()
    book_copies = []
    for ch in range(2):
        part = slice(ch * half_codes, (ch + 1) * half_codes)
        for jj, d in enumerate(routes):
            n_copy(jj, d, ch).wait()
            k_copy(jj, d, ch).wait()
        row = ksend[RING - 1, :, part]
        numerators = acc[part, 0:hd]
        for d in range(1, RING):
            row = row + kland[d - 1, :, part]
            numerators = numerators + nland[d - 1, part, :].astype(f32)
        new_counts = momentum * cnt_ref[:, part] + (1.0 - momentum) * row
        ncnt_ref[:, part] = new_counts
        inverse_counts = jnp.transpose(jnp.broadcast_to(1.0 / new_counts, (8, half_codes)))[:, 0:1]
        sums_buf[part, :] = (momentum * sums_buf[part, :] + (1.0 - momentum) * numerators) * inverse_counts
        book_copies.append(
            pltpu.make_async_copy(
                sums_buf.at[pl.ds(ch * half_codes, half_codes)],
                ncb_hbm.at[0, pl.ds(ch * half_codes, half_codes)],
                book_sem.at[ch],
            )
        )
        book_copies[-1].start()
    for d in range(1, heads):
        o_copy(d).wait()
    pltpu.make_async_copy(tsend.at[h], oland.at[h], own_sem).wait()
    c_copy(2).wait_send()
    for half in range(2):
        y_copy(2, half).wait_send()
    for copy in book_copies:
        copy.wait()


def place(oland, counts, book, quant_ref, ncnt_ref, ncb_ref):
    heads, _, hd = oland.shape
    for g in range(heads):
        quant_ref[:, g * hd:(g + 1) * hd] = oland[g]
    ncnt_ref[...] = counts[...]
    ncb_ref[...] = book[...]


def shards(tokens, codebook, ema_counts, ema_sums):
    heads = lax.axis_size("head")
    width, _ = tokens.shape
    _, codes, hd = codebook.shape
    rows = heads * width
    tile = rows // 2
    vmem = pl.BlockSpec(memory_space=pltpu.VMEM)
    dma = pltpu.SemaphoreType.DMA
    anywhere = pl.BlockSpec(memory_space=pl.ANY)
    far = RING - 1
    pieces, counts, book, _ = pl.pallas_call(
        functools.partial(kernel, heads),
        out_shape=(
            jax.ShapeDtypeStruct((heads, width, hd), bf16),
            jax.ShapeDtypeStruct(ema_counts.shape, f32),
            jax.ShapeDtypeStruct(ema_sums.shape, f32),
            jax.ShapeDtypeStruct((4 * RING, codes, tile), bf16),
        ),
        in_specs=[anywhere, anywhere, vmem, anywhere],
        out_specs=(anywhere, vmem, anywhere, anywhere),
        scratch_shapes=[
            pltpu.VMEM((4 * RING, codes, tile), bf16),
            pltpu.VMEM((2, codes, tile), f32),
            pltpu.VMEM((2, 1, tile), f32),
            pltpu.VMEM((RING, codes, hd), bf16),
            pltpu.VMEM((2, codes, hd), bf16),
            pltpu.VMEM((2, QROWS, codes), bf16),
            pltpu.VMEM((codes, hd), bf16),
            pltpu.VMEM((hd, codes), bf16),
            pltpu.VMEM(tokens.shape, bf16),
            pltpu.VMEM((heads, hd, width), bf16),
            pltpu.VMEM((RING, hd, rows), bf16),
            pltpu.VMEM((2 * RING, QROWS, tile), f32),
            pltpu.VMEM((RING, 8, tile), f32),
            pltpu.VMEM((far, RING, 8, tile), f32),
            pltpu.VMEM((RING, 2 * RING, tile), f32),
            pltpu.VMEM((RING, 2 * RING, tile), f32),
            pltpu.VMEM((RING, 8, tile), f32),
            pltpu.VMEM((RING, hd, rows), bf16),
            pltpu.VMEM((far, hd, rows), bf16),
            pltpu.VMEM((far, codes, hd), bf16),
            pltpu.VMEM((far, codes, hd), bf16),
            pltpu.VMEM((RING, 1, codes), f32),
            pltpu.VMEM((far, 1, codes), f32),
            dma((4 * RING,)),
            dma,
            dma,
            dma((2,)),
            dma((2,)),
            dma((far,)), dma((far,)),
            dma((max(heads - 1, 1),)), dma((max(heads - 1, 1),)),
            dma((2, far)), dma((2, far)),
            dma((RING, far)), dma((RING, far)),
            dma((far,)), dma((far,)),
            dma((max(heads - 1, 1),)), dma((max(heads - 1, 1),)),
            dma((far, 2)), dma((far, 2)),
            dma((far, 2)), dma((far, 2)),
        ],
        compiler_params=pltpu.CompilerParams(
            collective_id=0, has_side_effects=True, vmem_limit_bytes=63 * 2**20
        ),
    )(tokens, codebook, ema_counts, ema_sums)
    return pl.pallas_call(
        place,
        out_shape=(
            jax.ShapeDtypeStruct(tokens.shape, bf16),
            jax.ShapeDtypeStruct(ema_counts.shape, f32),
            jax.ShapeDtypeStruct(ema_sums.shape, f32),
        ),
        in_specs=[vmem] * 3,
        out_specs=(vmem,) * 3,
    )(pieces, counts, book)


def solution(mesh):
    placed = (
        P(("head", "code"), None),
        P("head", "code", None),
        P("head", "code"),
        P("head", "code", None),
    )
    return jax.shard_map(
        shards,
        mesh=mesh,
        in_specs=placed,
        out_specs=(P(("head", "code"), None), P("head", "code"), P("head", "code", None)),
        check_vma=False,
    )
```

```python
import functools

import jax
import jax.numpy as jnp
from jax import lax
from jax.experimental import pallas as pl
from jax.experimental.pallas import tpu as pltpu
from jax.sharding import PartitionSpec as P

MESH = pl.DeviceIdType.MESH
bf16 = jnp.bfloat16
f32 = jnp.float32
momentum = 0.8
half_log2e = 0.5 * 1.4426950408889634
RING = 4
QROWS = 144


def dot(a, b, ca, cb):
    return lax.dot_general(a, b, (((ca,), (cb,)), ((), ())), preferred_element_type=f32)


def gray(s):
    return s + (s // 2) * (1 - 2 * (s % 2))


def kernel(
    heads, tok_hbm, cb_hbm, cnt_ref, sums_hbm,
    oland, ncnt_ref, ncb_hbm, spill,
    e_buf, s_buf, m_buf, c_land, naug, c_t, naug_next, c_t_next, tok_ref, tsend, x_land, q_acc, stat, stat_land, mloc, f_buf, gain,
    qsend, qland, nsend, nland, ksend, kland,
    e_sem, sums_sem, own_sem, book_sem, in_sem, c_ss, c_rs, h_ss, h_rs, y_ss, y_rs, st_ss, st_rs, q_ss, q_rs, o_ss, o_rs, n_ss, n_rs, k_ss, k_rs,
):
    h = lax.axis_index("head")
    code = lax.axis_index("code")
    core = lax.rem(h, 2)
    first, second = code // RING, code % RING
    y = first * (1 - core) + second * core
    z = second * (1 - core) + first * core
    y_step, z_step = RING - (RING - 1) * core, 1 + (RING - 1) * core
    width = tok_ref.shape[0]
    codes, hd = cb_hbm.shape[1], cb_hbm.shape[2]
    tile = x_land.shape[2] // 2

    xs = heads // 2

    def from_head(k):
        return lax.rem(h // 2 + gray(k // 2), xs) * 2 + lax.rem(core + k % 2, 2)

    def to_head(k):
        return lax.rem(h // 2 + xs - gray(k // 2), xs) * 2 + lax.rem(core + k % 2, 2)

    def at_y(d):
        return (h, lax.rem(y + d, RING) * y_step + z * z_step)

    def at_z(d):
        return (h, y * y_step + lax.rem(z + d, RING) * z_step)

    def remote(src, dst, ss, rs, where):
        return pltpu.make_async_remote_copy(
            src_ref=src, dst_ref=dst, send_sem=ss, recv_sem=rs, device_id=where, device_id_type=MESH
        )

    sums_buf = s_buf.at[1, :, pl.ds(0, hd)]

    def sum_copy():
        return pltpu.make_async_copy(sums_hbm.at[0], sums_buf, sums_sem)

    tok_copy = pltpu.make_async_copy(tok_hbm, tok_ref, in_sem.at[0])
    tok_copy.start()
    own_codes = pltpu.make_async_copy(cb_hbm.at[0], c_land.at[z], in_sem.at[1])
    own_codes.start()

    barrier = pltpu.get_barrier_semaphore()
    for k in range(1, heads):
        pl.semaphore_signal(barrier, inc=1, device_id=(to_head(k), code), device_id_type=MESH)
    for d in range(1, RING):
        pl.semaphore_signal(barrier, inc=1, device_id=at_y(d), device_id_type=MESH)
        pl.semaphore_signal(barrier, inc=1, device_id=at_z(d), device_id_type=MESH)
    tok_copy.wait()
    for g in range(heads):
        block = tok_ref[:, g * hd:(g + 1) * hd].astype(f32)
        tsend[g] = jnp.transpose(block).astype(bf16)
    pl.semaphore_wait(barrier, heads - 1 + 2 * (RING - 1))

    def head_copy(k):
        head = to_head(k)
        other = lax.rem(head, 2)
        block = first * (1 - other) + second * other
        return remote(
            tsend.at[head], x_land.at[block, :, pl.ds(k * width, width)],
            h_ss.at[k - 1], h_rs.at[k - 1], (head, code),
        )

    def c_copy(d):
        return remote(cb_hbm.at[0], c_land.at[z], c_ss.at[d - 1], c_rs.at[d - 1], at_z(d))

    def y_copy(d, half):
        block = x_land.at[y, :, pl.ds(half * tile, tile)]
        return remote(block, block, y_ss.at[half, d - 1], y_rs.at[half, d - 1], at_y(d))

    for k in range(1, heads):
        head_copy(k).start()
    for d in (1, 3):
        c_copy(d).start()
    x_land[y, :, 0:width] = tsend[h]

    tail = lax.broadcasted_iota(jnp.int32, (QROWS - hd, codes), 0)
    for slot in range(2):
        c_t[slot, hd:, :] = jnp.where(tail == 0, 1.0, 0.0).astype(bf16)
    row = lax.broadcasted_iota(jnp.int32, (hd, tile), 0)
    ones_rows = jnp.where(row < 3, 1.0, 0.0).astype(bf16)

    def prepare(aug, cols, zb, start, count):
        part = pl.ds(start, count)
        c = c_land[zb, part, :].astype(f32)
        n = -0.5 * jnp.sum(c * c, axis=1, keepdims=True)
        hi = n.astype(bf16).astype(f32)
        rest = n - hi
        mid = rest.astype(bf16).astype(f32)
        low = rest - mid
        lane = lax.broadcasted_iota(jnp.int32, (count, hd), 1)
        aug[part, :] = jnp.where(lane == 0, hi, jnp.where(lane == 1, mid, jnp.where(lane == 2, low, 0.0))).astype(bf16)
        cols[0:hd, part] = jnp.transpose(c).astype(bf16)

    own_codes.wait()
    prepare(naug.at[0], c_t.at[0], z, 0, codes)
    stat[...] = jnp.full(stat.shape, -3e38, f32)
    q_acc[...] = jnp.zeros(q_acc.shape, f32)

    def row_block(j, s):
        first = 1 - (j + 3) // 4
        return lax.rem(first * (y + gray(s)) + (1 - first) * s, RING)

    def logits(j, s, half, slot):
        zb = lax.rem(z + gray(j), RING)
        yb = row_block(j, s)
        left = jnp.concatenate([c_land[zb], naug[j % 2]], axis=1)
        right = jnp.concatenate([x_land[yb, :, half * tile:(half + 1) * tile], ones_rows], axis=0)
        out = dot(left, right, 1, 0)
        s_buf[slot] = out
        m_buf[slot] = jnp.max(out, axis=0, keepdims=True)

    def finish(j, s, half, slot):
        yb = row_block(j, s)
        es = (j % 2) * (2 * RING) + 2 * s + half
        m = m_buf[slot]
        e = jnp.exp2((s_buf[slot] - m) * half_log2e).astype(bf16)
        e_buf[es] = e
        q = dot(c_t[j % 2], e, 1, 0)
        m_old = stat[yb, half:half + 1, :]
        m_new = jnp.maximum(m_old, m)
        q = q_acc[2 * yb + half] * jnp.exp2((m_old - m_new) * half_log2e) + q * jnp.exp2((m - m_new) * half_log2e)
        q_acc[2 * yb + half] = q
        stat[yb, half:half + 1, :] = m_new
        stat[yb, 2 + half:3 + half, :] = q[hd:hd + 1, :]
        mloc[yb, pl.ds(2 * j + half, 1), :] = m

    def spill_copy(es):
        return pltpu.make_async_copy(e_buf.at[es], spill.at[es], e_sem.at[es])

    def fetch_copy(es):
        return pltpu.make_async_copy(spill.at[es], e_buf.at[es], e_sem.at[es])

    def wait_rows(s, half):
        o = gray(s)
        block = x_land.at[lax.rem(y + o, RING), :, pl.ds(half * tile, tile)]
        remote(block, block, y_ss.at[half, 3 - o], y_rs.at[half, 3 - o], at_y(4 - o)).wait_recv()

    def wait_codes(j):
        o = gray(j)
        remote(
            cb_hbm.at[0], c_land.at[lax.rem(z + o, RING)], c_ss.at[3 - o], c_rs.at[3 - o], at_z(4 - o)
        ).wait_recv()

    def stat_copy(b, d):
        return remote(stat.at[b], stat_land.at[d - 1, b], st_ss.at[b, d - 1], st_rs.at[b, d - 1], at_y(d))

    pairs = RING * RING
    quarter = codes // RING

    for half in range(2):
        for k in range(max(1, half * heads // 2), (half + 1) * heads // 2):
            head_copy(k).wait()
        for d in (1, 3):
            y_copy(d, half).start()
        if half == 0:
            logits(0, 0, 0, 0)

    def first_step(p, late):
        @pl.when(p > 0)
        def _():
            wait_rows(p, 1)

        if late:
            @pl.when(p == 2)
            def _():
                for d in (1, 3):
                    c_copy(d).wait_send()
                c_copy(2).start()
                wait_codes(1)
        else:
            @pl.when(p == 1)
            def _():
                for half in range(2):
                    for d in (1, 3):
                        y_copy(d, half).wait_send()
                for half in range(2):
                    y_copy(2, half).start()

        logits(0, p, 1, 1)
        finish(0, p, 0, 0)
        if late:
            start = pl.multiple_of((p - 2) * (codes // 2), codes // 2)
            prepare(naug.at[1], c_t.at[1], lax.rem(z + 1, RING), start, codes // 2)

        @pl.when(p < RING - 1)
        def _():
            wait_rows(p + 1, 0)

        logits((p + 1) // RING, (p + 1) % RING, 0, 0)
        finish(0, p, 1, 1)
        spill_copy(2 * p).start()
        spill_copy(2 * p + 1).start()
        return 0

    def step(p, _):
        j, s = p // RING, p % RING
        pn = (p + 1) % pairs
        jn, sn = pn // RING, pn % RING
        es = (j % 2) * (2 * RING) + 2 * s

        @pl.when((s == 0) & (j < RING - 1))
        def _():
            wait_codes(j + 1)

        ahead = lax.rem(z + gray((j + 1) % RING), RING)

        @pl.when((s == RING - 1) & (j < RING - 1))
        def _():
            slot = (j + 1) % 2
            done = (RING - 1) * quarter
            naug[slot, 0:done, :] = naug_next[0:done, :]
            c_t[slot, 0:hd, 0:done] = c_t_next[0:hd, 0:done]
            prepare(naug.at[slot], c_t.at[slot], ahead, done, quarter)

        @pl.when(j >= 2)
        def _():
            spill_copy(es).wait()
            spill_copy(es + 1).wait()

        logits(j, s, 1, 1)
        finish(j, s, 0, 0)
        logits(jn, sn, 0, 0)
        finish(j, s, 1, 1)
        prepare(naug_next, c_t_next, ahead, pl.multiple_of(s * quarter, quarter), quarter)

        @pl.when(j == RING - 1)
        def _():
            for d in range(1, RING):
                stat_copy(s, d).start()

        @pl.when(j < 2)
        def _():
            spill_copy(es).start()
            spill_copy(es + 1).start()

        return 0

    lax.fori_loop(0, 2, lambda p, _: first_step(p, False), 0)
    lax.fori_loop(2, RING, lambda p, _: first_step(p, True), 0)
    lax.fori_loop(RING, pairs, step, 0)
    sum_copy().start()

    def q_copy(b):
        d = lax.rem(b - y + RING, RING)
        return remote(qsend.at[b], qland.at[d - 1], q_ss.at[d - 1], q_rs.at[d - 1], (h, b * y_step + z * z_step))

    def q_wait(d):
        b = lax.rem(y + d, RING)
        return remote(qsend.at[b], qland.at[d - 1], q_ss.at[d - 1], q_rs.at[d - 1], (h, b * y_step + z * z_step))

    def totals(b):
        for d in range(1, RING):
            stat_copy(b, d).wait()
        m, l = stat[b, 0:2, :], stat[b, 2:4, :]
        top = m
        for d in range(1, RING):
            top = jnp.maximum(top, stat_land[d - 1, b, 0:2, :])
        total = l * jnp.exp2((m - top) * half_log2e)
        for d in range(1, RING):
            total = total + stat_land[d - 1, b, 2:4, :] * jnp.exp2((stat_land[d - 1, b, 0:2, :] - top) * half_log2e)
        inverse = 1.0 / total
        gain[b, 0:2, :] = jnp.exp2((m - top) * half_log2e) * inverse
        even = lax.broadcasted_iota(jnp.int32, (2 * RING, tile), 0) % 2 == 0
        top_all = jnp.where(even, top[0:1, :], top[1:2, :])
        f_buf[b] = jnp.exp2((mloc[b] - top_all) * half_log2e) * jnp.where(even, inverse[0:1, :], inverse[1:2, :])

    def quantized_rows(b):
        for half in range(2):
            cols = slice(half * tile, (half + 1) * tile)
            qsend[b, :, cols] = (q_acc[2 * b + half, 0:hd, :] * gain[b, half:half + 1, :]).astype(bf16)

    def send_rows(b):
        @pl.when(y != b)
        def _():
            q_copy(b).start()

    def o_copy(k):
        return remote(tsend.at[k], oland.at[h], o_ss.at[k - 1], o_rs.at[k - 1], (from_head(k), code))

    def quantized_part(part):
        for g in range(heads // 2):
            k = (heads // 2) * part + g
            cols = pl.ds(pl.multiple_of(k * width, 128), width)
            block = qsend[y, :, cols].astype(f32)
            for d in range(1, RING):
                block = block + qland[d - 1, :, cols].astype(f32)
            tsend[k] = jnp.transpose(block).astype(bf16)

    def send_quantized():
        for k in range(1, heads):
            o_copy(k).start()
        pltpu.make_async_copy(tsend.at[0], oland.at[h], own_sem).start()

    group = 4
    half_codes = codes // 2
    acc = s_buf.at[0, :, pl.ds(0, 2 * hd)]
    pad_row = lax.broadcasted_iota(jnp.int32, (hd, tile), 0)

    def via(d):
        return at_z(1 if d == 2 else d)

    def n_copy(jj, d, ch):
        part = pl.ds(pl.multiple_of(ch * half_codes, half_codes), half_codes)
        return remote(nsend.at[jj, part], nland.at[d - 1, part], n_ss.at[d - 1, ch], n_rs.at[d - 1, ch], via(d))

    def k_copy(jj, d, ch):
        part = pl.ds(pl.multiple_of(ch * half_codes, half_codes), half_codes)
        return remote(
            ksend.at[jj, :, part], kland.at[d - 1, :, part], k_ss.at[d - 1, ch], k_rs.at[d - 1, ch], via(d)
        )

    def scaled(j, t):
        yb = row_block(j, t // 2)
        f = f_buf[yb, 2 * j + t % 2:2 * j + t % 2 + 1, :]
        x = x_land[yb, :, (t % 2) * tile:(t % 2 + 1) * tile].astype(f32)
        f_hi = f.astype(bf16).astype(f32)
        extra = jnp.where(pad_row == 0, f_hi, jnp.where(pad_row == 1, f - f_hi, 0.0))
        return jnp.concatenate([(x * f).astype(bf16), extra.astype(bf16)], axis=0)

    routes = (2, 3, 1)
    for jj in range(RING):
        j = RING - 1 - jj
        base = (j % 2) * (2 * RING)
        for g in range(2 * RING // group):
            tiles = range(g * group, (g + 1) * group)
            if jj == 0:
                for b in range(g * group // 2, (g + 1) * group // 2):
                    totals(b)
            if jj >= 2:
                for t in tiles:
                    fetch_copy(base + t).wait()
            if j == 0 and g == 0:
                for d in range(1, RING):
                    q_wait(d).wait()

            if jj == 2 and g > 0:
                for ch in range(2):
                    n_copy(0, 2, ch).wait()
                    k_copy(0, 2, ch).wait()

            def some_codes(ch, _, j=j, jj=jj, base=base, tiles=tiles, g=g):
                part = pl.ds(pl.multiple_of(ch * half_codes, half_codes), half_codes)
                left = jnp.concatenate([e_buf[base + t, part, :] for t in tiles], axis=1)
                right = jnp.concatenate([scaled(j, t) for t in tiles], axis=1)
                out = dot(left, right, 1, 1)
                if jj == 0:
                    quantized_rows(2 * g + ch)
                if j == 0 and g == 0:
                    quantized_part(ch)
                if g > 0:
                    out = out + acc[part, :]
                if g < 2 * RING // group - 1:
                    acc[part, :] = out
                else:
                    columns = jnp.transpose(out[:, hd:2 * hd])
                    row = columns[0:1, :] + columns[1:2, :]
                    numer = out[:, 0:hd]
                    if jj == 2:
                        row = row + kland[1, :, part]
                        numer = numer + nland[1, part, :].astype(f32)
                    ksend[jj, :, part] = row
                    if j > 0:
                        nsend[jj, part, :] = numer.astype(bf16)
                        n_copy(jj, routes[jj], ch).start()
                        k_copy(jj, routes[jj], ch).start()
                    else:
                        acc[part, 0:hd] = numer
                if jj == 0:
                    send_rows(2 * g + ch)
                return 0

            lax.fori_loop(0, 2, some_codes, 0)
            if jj < 2:
                for t in tiles:
                    fetch_copy(base + t).start()
            if j == 0 and g == 0:
                send_quantized()

    sum_copy().wait()
    book_copies = []
    for ch in range(2):
        part = slice(ch * half_codes, (ch + 1) * half_codes)
        for jj, d in ((1, 3), (2, 1)):
            n_copy(jj, d, ch).wait()
            k_copy(jj, d, ch).wait()
        row = ksend[RING - 1, :, part]
        numerators = acc[part, 0:hd]
        for d in (1, 3):
            row = row + kland[d - 1, :, part]
            numerators = numerators + nland[d - 1, part, :].astype(f32)
        new_counts = momentum * cnt_ref[:, part] + (1.0 - momentum) * row
        ncnt_ref[:, part] = new_counts
        inverse_counts = jnp.transpose(jnp.broadcast_to(1.0 / new_counts, (8, half_codes)))[:, 0:1]
        sums_buf[part, :] = (momentum * sums_buf[part, :] + (1.0 - momentum) * numerators) * inverse_counts
        book_copies.append(
            pltpu.make_async_copy(
                sums_buf.at[pl.ds(ch * half_codes, half_codes)],
                ncb_hbm.at[0, pl.ds(ch * half_codes, half_codes)],
                book_sem.at[ch],
            )
        )
        book_copies[-1].start()
    for k in range(1, heads):
        o_copy(k).wait()
    pltpu.make_async_copy(tsend.at[0], oland.at[h], own_sem).wait()
    c_copy(2).wait_send()
    for half in range(2):
        y_copy(2, half).wait_send()
    for copy in book_copies:
        copy.wait()


def place(oland, counts, book, quant_ref, ncnt_ref, ncb_ref):
    heads, _, hd = oland.shape
    for g in range(heads):
        quant_ref[:, g * hd:(g + 1) * hd] = oland[g]
    ncnt_ref[...] = counts[...]
    ncb_ref[...] = book[...]


def shards(tokens, codebook, ema_counts, ema_sums):
    heads = lax.axis_size("head")
    width, _ = tokens.shape
    _, codes, hd = codebook.shape
    rows = heads * width
    tile = rows // 2
    vmem = pl.BlockSpec(memory_space=pltpu.VMEM)
    dma = pltpu.SemaphoreType.DMA
    anywhere = pl.BlockSpec(memory_space=pl.ANY)
    far = RING - 1
    pieces, counts, book, _ = pl.pallas_call(
        functools.partial(kernel, heads),
        out_shape=(
            jax.ShapeDtypeStruct((heads, width, hd), bf16),
            jax.ShapeDtypeStruct(ema_counts.shape, f32),
            jax.ShapeDtypeStruct(ema_sums.shape, f32),
            jax.ShapeDtypeStruct((4 * RING, codes, tile), bf16),
        ),
        in_specs=[anywhere, anywhere, vmem, anywhere],
        out_specs=(anywhere, vmem, anywhere, anywhere),
        scratch_shapes=[
            pltpu.VMEM((4 * RING, codes, tile), bf16),
            pltpu.VMEM((2, codes, tile), f32),
            pltpu.VMEM((2, 1, tile), f32),
            pltpu.VMEM((RING, codes, hd), bf16),
            pltpu.VMEM((2, codes, hd), bf16),
            pltpu.VMEM((2, QROWS, codes), bf16),
            pltpu.VMEM((codes, hd), bf16),
            pltpu.VMEM((hd, codes), bf16),
            pltpu.VMEM(tokens.shape, bf16),
            pltpu.VMEM((heads, hd, width), bf16),
            pltpu.VMEM((RING, hd, rows), bf16),
            pltpu.VMEM((2 * RING, QROWS, tile), f32),
            pltpu.VMEM((RING, 8, tile), f32),
            pltpu.VMEM((far, RING, 8, tile), f32),
            pltpu.VMEM((RING, 2 * RING, tile), f32),
            pltpu.VMEM((RING, 2 * RING, tile), f32),
            pltpu.VMEM((RING, 8, tile), f32),
            pltpu.VMEM((RING, hd, rows), bf16),
            pltpu.VMEM((far, hd, rows), bf16),
            pltpu.VMEM((far, codes, hd), bf16),
            pltpu.VMEM((far, codes, hd), bf16),
            pltpu.VMEM((RING, 1, codes), f32),
            pltpu.VMEM((far, 1, codes), f32),
            dma((4 * RING,)),
            dma,
            dma,
            dma((2,)),
            dma((2,)),
            dma((far,)), dma((far,)),
            dma((max(heads - 1, 1),)), dma((max(heads - 1, 1),)),
            dma((2, far)), dma((2, far)),
            dma((RING, far)), dma((RING, far)),
            dma((far,)), dma((far,)),
            dma((max(heads - 1, 1),)), dma((max(heads - 1, 1),)),
            dma((far, 2)), dma((far, 2)),
            dma((far, 2)), dma((far, 2)),
        ],
        compiler_params=pltpu.CompilerParams(
            collective_id=0, has_side_effects=True, vmem_limit_bytes=63 * 2**20
        ),
    )(tokens, codebook, ema_counts, ema_sums)
    return pl.pallas_call(
        place,
        out_shape=(
            jax.ShapeDtypeStruct(tokens.shape, bf16),
            jax.ShapeDtypeStruct(ema_counts.shape, f32),
            jax.ShapeDtypeStruct(ema_sums.shape, f32),
        ),
        in_specs=[vmem] * 3,
        out_specs=(vmem,) * 3,
    )(pieces, counts, book)


def solution(mesh):
    placed = (
        P(("head", "code"), None),
        P("head", "code", None),
        P("head", "code"),
        P("head", "code", None),
    )
    return jax.shard_map(
        shards,
        mesh=mesh,
        in_specs=placed,
        out_specs=(P(("head", "code"), None), P("head", "code"), P("head", "code", None)),
        check_vma=False,
    )
```

```python
import functools

import jax
import jax.numpy as jnp
from jax import lax
from jax.experimental import pallas as pl
from jax.experimental.pallas import tpu as pltpu
from jax.sharding import PartitionSpec as P

MESH = pl.DeviceIdType.MESH
bf16 = jnp.bfloat16
f32 = jnp.float32
momentum = 0.8
half_log2e = 0.5 * 1.4426950408889634
RING = 4
QROWS = 144


def dot(a, b, ca, cb):
    return lax.dot_general(a, b, (((ca,), (cb,)), ((), ())), preferred_element_type=f32)


def gray(s):
    return s + (s // 2) * (1 - 2 * (s % 2))


def kernel(
    heads, tok_hbm, cb_hbm, cnt_ref, sums_hbm,
    oland, ncnt_ref, ncb_hbm, spill,
    e_buf, s_buf, m_buf, c_land, naug, c_t, naug_next, c_t_next, tok_ref, tsend, x_land, q_acc, stat, stat_land, mloc, f_buf, gain,
    qsend, qland, nsend, nland, ksend, kland,
    e_sem, sums_sem, own_sem, book_sem, in_sem, c_ss, c_rs, h_ss, h_rs, y_ss, y_rs, st_ss, st_rs, q_ss, q_rs, o_ss, o_rs, n_ss, n_rs, k_ss, k_rs,
):
    h = lax.axis_index("head")
    code = lax.axis_index("code")
    core = lax.rem(h, 2)
    first, second = code // RING, code % RING
    y = first * (1 - core) + second * core
    z = second * (1 - core) + first * core
    y_step, z_step = RING - (RING - 1) * core, 1 + (RING - 1) * core
    width = tok_ref.shape[0]
    codes, hd = cb_hbm.shape[1], cb_hbm.shape[2]
    tile = x_land.shape[2] // 2

    xs = heads // 2

    def from_head(k):
        return lax.rem(h // 2 + gray(k // 2), xs) * 2 + lax.rem(core + k % 2, 2)

    def to_head(k):
        return lax.rem(h // 2 + xs - gray(k // 2), xs) * 2 + lax.rem(core + k % 2, 2)

    def at_y(d):
        return (h, lax.rem(y + d, RING) * y_step + z * z_step)

    def at_z(d):
        return (h, y * y_step + lax.rem(z + d, RING) * z_step)

    def remote(src, dst, ss, rs, where):
        return pltpu.make_async_remote_copy(
            src_ref=src, dst_ref=dst, send_sem=ss, recv_sem=rs, device_id=where, device_id_type=MESH
        )

    sums_buf = s_buf.at[1, :, pl.ds(0, hd)]

    def sum_copy():
        return pltpu.make_async_copy(sums_hbm.at[0], sums_buf, sums_sem)

    tok_copy = pltpu.make_async_copy(tok_hbm, tok_ref, in_sem.at[0])
    tok_copy.start()
    own_codes = pltpu.make_async_copy(cb_hbm.at[0], c_land.at[z], in_sem.at[1])
    own_codes.start()

    barrier = pltpu.get_barrier_semaphore()
    for k in range(1, heads):
        pl.semaphore_signal(barrier, inc=1, device_id=(to_head(k), code), device_id_type=MESH)
    for d in range(1, RING):
        pl.semaphore_signal(barrier, inc=1, device_id=at_y(d), device_id_type=MESH)
        pl.semaphore_signal(barrier, inc=1, device_id=at_z(d), device_id_type=MESH)
    tok_copy.wait()
    for g in range(heads):
        block = tok_ref[:, g * hd:(g + 1) * hd].astype(f32)
        tsend[g] = jnp.transpose(block).astype(bf16)
    pl.semaphore_wait(barrier, heads - 1 + 2 * (RING - 1))

    def head_copy(k):
        head = to_head(k)
        other = lax.rem(head, 2)
        block = first * (1 - other) + second * other
        return remote(
            tsend.at[head], x_land.at[block, :, pl.ds(k * width, width)],
            h_ss.at[k - 1], h_rs.at[k - 1], (head, code),
        )

    def c_copy(d):
        return remote(cb_hbm.at[0], c_land.at[z], c_ss.at[d - 1], c_rs.at[d - 1], at_z(d))

    def y_copy(d, half):
        block = x_land.at[y, :, pl.ds(half * tile, tile)]
        return remote(block, block, y_ss.at[half, d - 1], y_rs.at[half, d - 1], at_y(d))

    for k in range(1, heads):
        head_copy(k).start()
    for d in (1, 3):
        c_copy(d).start()
    x_land[y, :, 0:width] = tsend[h]

    tail = lax.broadcasted_iota(jnp.int32, (QROWS - hd, codes), 0)
    for slot in range(2):
        c_t[slot, hd:, :] = jnp.where(tail == 0, 1.0, 0.0).astype(bf16)
    row = lax.broadcasted_iota(jnp.int32, (hd, tile), 0)
    ones_rows = jnp.where(row < 3, 1.0, 0.0).astype(bf16)

    def prepare(aug, cols, zb, start, count):
        part = pl.ds(start, count)
        c = c_land[zb, part, :].astype(f32)
        n = -0.5 * jnp.sum(c * c, axis=1, keepdims=True)
        hi = n.astype(bf16).astype(f32)
        rest = n - hi
        mid = rest.astype(bf16).astype(f32)
        low = rest - mid
        lane = lax.broadcasted_iota(jnp.int32, (count, hd), 1)
        aug[part, :] = jnp.where(lane == 0, hi, jnp.where(lane == 1, mid, jnp.where(lane == 2, low, 0.0))).astype(bf16)
        cols[0:hd, part] = jnp.transpose(c).astype(bf16)

    own_codes.wait()
    prepare(naug.at[0], c_t.at[0], z, 0, codes)
    stat[...] = jnp.full(stat.shape, -3e38, f32)
    q_acc[...] = jnp.zeros(q_acc.shape, f32)

    def row_block(j, s):
        first = 1 - (j + 3) // 4
        return lax.rem(first * (y + gray(s)) + (1 - first) * s, RING)

    def logits(j, s, half, slot):
        zb = lax.rem(z + gray(j), RING)
        yb = row_block(j, s)
        left = jnp.concatenate([c_land[zb], naug[j % 2]], axis=1)
        right = jnp.concatenate([x_land[yb, :, half * tile:(half + 1) * tile], ones_rows], axis=0)
        out = dot(left, right, 1, 0)
        s_buf[slot] = out
        m_buf[slot] = jnp.max(out, axis=0, keepdims=True)

    def finish(j, s, half, slot):
        yb = row_block(j, s)
        es = (j % 2) * (2 * RING) + 2 * s + half
        m = m_buf[slot]
        e = jnp.exp2((s_buf[slot] - m) * half_log2e).astype(bf16)
        e_buf[es] = e
        q = dot(c_t[j % 2], e, 1, 0)
        m_old = stat[yb, half:half + 1, :]
        m_new = jnp.maximum(m_old, m)
        q = q_acc[2 * yb + half] * jnp.exp2((m_old - m_new) * half_log2e) + q * jnp.exp2((m - m_new) * half_log2e)
        q_acc[2 * yb + half] = q
        stat[yb, half:half + 1, :] = m_new
        stat[yb, 2 + half:3 + half, :] = q[hd:hd + 1, :]
        mloc[yb, pl.ds(2 * j + half, 1), :] = m

    def spill_copy(es):
        return pltpu.make_async_copy(e_buf.at[es], spill.at[es], e_sem.at[es])

    def fetch_copy(es):
        return pltpu.make_async_copy(spill.at[es], e_buf.at[es], e_sem.at[es])

    def wait_rows(s, half):
        o = gray(s)
        block = x_land.at[lax.rem(y + o, RING), :, pl.ds(half * tile, tile)]
        remote(block, block, y_ss.at[half, 3 - o], y_rs.at[half, 3 - o], at_y(4 - o)).wait_recv()

    def wait_codes(j):
        o = gray(j)
        remote(
            cb_hbm.at[0], c_land.at[lax.rem(z + o, RING)], c_ss.at[3 - o], c_rs.at[3 - o], at_z(4 - o)
        ).wait_recv()

    def stat_copy(b, d):
        return remote(stat.at[b], stat_land.at[d - 1, b], st_ss.at[b, d - 1], st_rs.at[b, d - 1], at_y(d))

    pairs = RING * RING
    quarter = codes // RING

    for half in range(2):
        for k in range(max(1, half * heads // 2), (half + 1) * heads // 2):
            head_copy(k).wait()
        for d in (1, 3):
            y_copy(d, half).start()
        if half == 0:
            logits(0, 0, 0, 0)
    for half in range(2):
        y_copy(2, half).start()

    def first_step(p, late):
        @pl.when(p > 0)
        def _():
            wait_rows(p, 1)

        if late:
            @pl.when(p == 2)
            def _():
                for d in (1, 3):
                    c_copy(d).wait_send()
                c_copy(2).start()
                wait_codes(1)

        logits(0, p, 1, 1)
        finish(0, p, 0, 0)
        if late:
            start = pl.multiple_of((p - 2) * (codes // 2), codes // 2)
            prepare(naug.at[1], c_t.at[1], lax.rem(z + 1, RING), start, codes // 2)

        @pl.when(p < RING - 1)
        def _():
            wait_rows(p + 1, 0)

        logits((p + 1) // RING, (p + 1) % RING, 0, 0)
        finish(0, p, 1, 1)
        spill_copy(2 * p).start()
        spill_copy(2 * p + 1).start()
        return 0

    def step(p, _):
        j, s = p // RING, p % RING
        pn = (p + 1) % pairs
        jn, sn = pn // RING, pn % RING
        es = (j % 2) * (2 * RING) + 2 * s

        @pl.when((s == 0) & (j < RING - 1))
        def _():
            wait_codes(j + 1)

        ahead = lax.rem(z + gray((j + 1) % RING), RING)

        @pl.when((s == RING - 1) & (j < RING - 1))
        def _():
            slot = (j + 1) % 2
            done = (RING - 1) * quarter
            naug[slot, 0:done, :] = naug_next[0:done, :]
            c_t[slot, 0:hd, 0:done] = c_t_next[0:hd, 0:done]
            prepare(naug.at[slot], c_t.at[slot], ahead, done, quarter)

        @pl.when(j >= 2)
        def _():
            spill_copy(es).wait()
            spill_copy(es + 1).wait()

        logits(j, s, 1, 1)
        finish(j, s, 0, 0)
        logits(jn, sn, 0, 0)
        finish(j, s, 1, 1)
        prepare(naug_next, c_t_next, ahead, pl.multiple_of(s * quarter, quarter), quarter)

        @pl.when(j == RING - 1)
        def _():
            for d in range(1, RING):
                stat_copy(s, d).start()

        @pl.when(j < 2)
        def _():
            spill_copy(es).start()
            spill_copy(es + 1).start()

        return 0

    lax.fori_loop(0, 2, lambda p, _: first_step(p, False), 0)
    lax.fori_loop(2, RING, lambda p, _: first_step(p, True), 0)
    lax.fori_loop(RING, pairs, step, 0)
    sum_copy().start()

    def q_copy(b):
        d = lax.rem(b - y + RING, RING)
        return remote(qsend.at[b], qland.at[d - 1], q_ss.at[d - 1], q_rs.at[d - 1], (h, b * y_step + z * z_step))

    def q_wait(d):
        b = lax.rem(y + d, RING)
        return remote(qsend.at[b], qland.at[d - 1], q_ss.at[d - 1], q_rs.at[d - 1], (h, b * y_step + z * z_step))

    def totals(b):
        for d in range(1, RING):
            stat_copy(b, d).wait()
        m, l = stat[b, 0:2, :], stat[b, 2:4, :]
        top = m
        for d in range(1, RING):
            top = jnp.maximum(top, stat_land[d - 1, b, 0:2, :])
        total = l * jnp.exp2((m - top) * half_log2e)
        for d in range(1, RING):
            total = total + stat_land[d - 1, b, 2:4, :] * jnp.exp2((stat_land[d - 1, b, 0:2, :] - top) * half_log2e)
        inverse = 1.0 / total
        gain[b, 0:2, :] = jnp.exp2((m - top) * half_log2e) * inverse
        even = lax.broadcasted_iota(jnp.int32, (2 * RING, tile), 0) % 2 == 0
        top_all = jnp.where(even, top[0:1, :], top[1:2, :])
        f_buf[b] = jnp.exp2((mloc[b] - top_all) * half_log2e) * jnp.where(even, inverse[0:1, :], inverse[1:2, :])

    def quantized_rows(b):
        for half in range(2):
            cols = slice(half * tile, (half + 1) * tile)
            qsend[b, :, cols] = (q_acc[2 * b + half, 0:hd, :] * gain[b, half:half + 1, :]).astype(bf16)

    def send_rows(b):
        @pl.when(y != b)
        def _():
            q_copy(b).start()

    def o_copy(k):
        return remote(tsend.at[k], oland.at[h], o_ss.at[k - 1], o_rs.at[k - 1], (from_head(k), code))

    def quantized_part(part):
        for g in range(heads // 2):
            k = (heads // 2) * part + g
            cols = pl.ds(pl.multiple_of(k * width, 128), width)
            block = qsend[y, :, cols].astype(f32)
            for d in range(1, RING):
                block = block + qland[d - 1, :, cols].astype(f32)
            tsend[k] = jnp.transpose(block).astype(bf16)

    def send_quantized():
        for k in range(1, heads):
            o_copy(k).start()
        pltpu.make_async_copy(tsend.at[0], oland.at[h], own_sem).start()

    group = 4
    half_codes = codes // 2
    acc = s_buf.at[0, :, pl.ds(0, 2 * hd)]
    pad_row = lax.broadcasted_iota(jnp.int32, (hd, tile), 0)

    def via(d):
        return at_z(1 if d == 2 else d)

    def n_copy(jj, d, ch):
        part = pl.ds(pl.multiple_of(ch * half_codes, half_codes), half_codes)
        return remote(nsend.at[jj, part], nland.at[d - 1, part], n_ss.at[d - 1, ch], n_rs.at[d - 1, ch], via(d))

    def k_copy(jj, d, ch):
        part = pl.ds(pl.multiple_of(ch * half_codes, half_codes), half_codes)
        return remote(
            ksend.at[jj, :, part], kland.at[d - 1, :, part], k_ss.at[d - 1, ch], k_rs.at[d - 1, ch], via(d)
        )

    def scaled(j, t):
        yb = row_block(j, t // 2)
        f = f_buf[yb, 2 * j + t % 2:2 * j + t % 2 + 1, :]
        x = x_land[yb, :, (t % 2) * tile:(t % 2 + 1) * tile].astype(f32)
        f_hi = f.astype(bf16).astype(f32)
        extra = jnp.where(pad_row == 0, f_hi, jnp.where(pad_row == 1, f - f_hi, 0.0))
        return jnp.concatenate([(x * f).astype(bf16), extra.astype(bf16)], axis=0)

    routes = (2, 3, 1)
    for jj in range(RING):
        j = RING - 1 - jj
        base = (j % 2) * (2 * RING)
        for g in range(2 * RING // group):
            tiles = range(g * group, (g + 1) * group)
            if jj == 0:
                for b in range(g * group // 2, (g + 1) * group // 2):
                    totals(b)
            if jj >= 2:
                for t in tiles:
                    fetch_copy(base + t).wait()
            if j == 0 and g == 0:
                for d in range(1, RING):
                    q_wait(d).wait()

            if j == 0 and g > 0:
                for ch in range(2):
                    n_copy(1, 3, ch).wait()
                    k_copy(1, 3, ch).wait()
            if jj == 2 and g > 0:
                for ch in range(2):
                    n_copy(0, 2, ch).wait()
                    k_copy(0, 2, ch).wait()

            def some_codes(ch, _, j=j, jj=jj, base=base, tiles=tiles, g=g):
                part = pl.ds(pl.multiple_of(ch * half_codes, half_codes), half_codes)
                left = jnp.concatenate([e_buf[base + t, part, :] for t in tiles], axis=1)
                right = jnp.concatenate([scaled(j, t) for t in tiles], axis=1)
                out = dot(left, right, 1, 1)
                if jj == 0:
                    quantized_rows(2 * g + ch)
                if j == 0 and g == 0:
                    quantized_part(ch)
                if g > 0:
                    out = out + acc[part, :]
                if g < 2 * RING // group - 1:
                    acc[part, :] = out
                else:
                    columns = jnp.transpose(out[:, hd:2 * hd])
                    row = columns[0:1, :] + columns[1:2, :]
                    numer = out[:, 0:hd]
                    if jj >= 2:
                        row = row + kland[jj - 1, :, part]
                        numer = numer + nland[jj - 1, part, :].astype(f32)
                    ksend[jj, :, part] = row
                    if j > 0:
                        nsend[jj, part, :] = numer.astype(bf16)
                        n_copy(jj, routes[jj], ch).start()
                        k_copy(jj, routes[jj], ch).start()
                    else:
                        acc[part, 0:hd] = numer
                if jj == 0:
                    send_rows(2 * g + ch)
                return 0

            lax.fori_loop(0, 2, some_codes, 0)
            if jj < 2:
                for t in tiles:
                    fetch_copy(base + t).start()
            if j == 0 and g == 0:
                send_quantized()

    sum_copy().wait()
    book_copies = []
    for ch in range(2):
        part = slice(ch * half_codes, (ch + 1) * half_codes)
        n_copy(2, 1, ch).wait()
        k_copy(2, 1, ch).wait()
        row = ksend[RING - 1, :, part] + kland[0, :, part]
        numerators = acc[part, 0:hd] + nland[0, part, :].astype(f32)
        new_counts = momentum * cnt_ref[:, part] + (1.0 - momentum) * row
        ncnt_ref[:, part] = new_counts
        inverse_counts = jnp.transpose(jnp.broadcast_to(1.0 / new_counts, (8, half_codes)))[:, 0:1]
        sums_buf[part, :] = (momentum * sums_buf[part, :] + (1.0 - momentum) * numerators) * inverse_counts
        book_copies.append(
            pltpu.make_async_copy(
                sums_buf.at[pl.ds(ch * half_codes, half_codes)],
                ncb_hbm.at[0, pl.ds(ch * half_codes, half_codes)],
                book_sem.at[ch],
            )
        )
        book_copies[-1].start()
    for k in range(1, heads):
        o_copy(k).wait()
    pltpu.make_async_copy(tsend.at[0], oland.at[h], own_sem).wait()
    c_copy(2).wait_send()
    for half in range(2):
        for d in range(1, RING):
            y_copy(d, half).wait_send()
    for copy in book_copies:
        copy.wait()


def place(oland, counts, book, quant_ref, ncnt_ref, ncb_ref):
    heads, _, hd = oland.shape
    for g in range(heads):
        quant_ref[:, g * hd:(g + 1) * hd] = oland[g]
    ncnt_ref[...] = counts[...]
    ncb_ref[...] = book[...]


def shards(tokens, codebook, ema_counts, ema_sums):
    heads = lax.axis_size("head")
    width, _ = tokens.shape
    _, codes, hd = codebook.shape
    rows = heads * width
    tile = rows // 2
    vmem = pl.BlockSpec(memory_space=pltpu.VMEM)
    dma = pltpu.SemaphoreType.DMA
    anywhere = pl.BlockSpec(memory_space=pl.ANY)
    far = RING - 1
    pieces, counts, book, _ = pl.pallas_call(
        functools.partial(kernel, heads),
        out_shape=(
            jax.ShapeDtypeStruct((heads, width, hd), bf16),
            jax.ShapeDtypeStruct(ema_counts.shape, f32),
            jax.ShapeDtypeStruct(ema_sums.shape, f32),
            jax.ShapeDtypeStruct((4 * RING, codes, tile), bf16),
        ),
        in_specs=[anywhere, anywhere, vmem, anywhere],
        out_specs=(anywhere, vmem, anywhere, anywhere),
        scratch_shapes=[
            pltpu.VMEM((4 * RING, codes, tile), bf16),
            pltpu.VMEM((2, codes, tile), f32),
            pltpu.VMEM((2, 1, tile), f32),
            pltpu.VMEM((RING, codes, hd), bf16),
            pltpu.VMEM((2, codes, hd), bf16),
            pltpu.VMEM((2, QROWS, codes), bf16),
            pltpu.VMEM((codes, hd), bf16),
            pltpu.VMEM((hd, codes), bf16),
            pltpu.VMEM(tokens.shape, bf16),
            pltpu.VMEM((heads, hd, width), bf16),
            pltpu.VMEM((RING, hd, rows), bf16),
            pltpu.VMEM((2 * RING, QROWS, tile), f32),
            pltpu.VMEM((RING, 8, tile), f32),
            pltpu.VMEM((far, RING, 8, tile), f32),
            pltpu.VMEM((RING, 2 * RING, tile), f32),
            pltpu.VMEM((RING, 2 * RING, tile), f32),
            pltpu.VMEM((RING, 8, tile), f32),
            pltpu.VMEM((RING, hd, rows), bf16),
            pltpu.VMEM((far, hd, rows), bf16),
            pltpu.VMEM((far, codes, hd), bf16),
            pltpu.VMEM((far, codes, hd), bf16),
            pltpu.VMEM((RING, 1, codes), f32),
            pltpu.VMEM((far, 1, codes), f32),
            dma((4 * RING,)),
            dma,
            dma,
            dma((2,)),
            dma((2,)),
            dma((far,)), dma((far,)),
            dma((max(heads - 1, 1),)), dma((max(heads - 1, 1),)),
            dma((2, far)), dma((2, far)),
            dma((RING, far)), dma((RING, far)),
            dma((far,)), dma((far,)),
            dma((max(heads - 1, 1),)), dma((max(heads - 1, 1),)),
            dma((far, 2)), dma((far, 2)),
            dma((far, 2)), dma((far, 2)),
        ],
        compiler_params=pltpu.CompilerParams(
            collective_id=0, has_side_effects=True, vmem_limit_bytes=63 * 2**20
        ),
    )(tokens, codebook, ema_counts, ema_sums)
    return pl.pallas_call(
        place,
        out_shape=(
            jax.ShapeDtypeStruct(tokens.shape, bf16),
            jax.ShapeDtypeStruct(ema_counts.shape, f32),
            jax.ShapeDtypeStruct(ema_sums.shape, f32),
        ),
        grid=(2,),
        in_specs=[
            pl.BlockSpec((heads // 2, width, hd), lambda i: (i, 0, 0)),
            pl.BlockSpec((1, codes // 2), lambda i: (0, i)),
            pl.BlockSpec((1, codes // 2, hd), lambda i: (0, i, 0)),
        ],
        out_specs=(
            pl.BlockSpec((width, heads // 2 * hd), lambda i: (0, i)),
            pl.BlockSpec((1, codes // 2), lambda i: (0, i)),
            pl.BlockSpec((1, codes // 2, hd), lambda i: (0, i, 0)),
        ),
    )(pieces, counts, book)


def solution(mesh):
    placed = (
        P(("head", "code"), None),
        P("head", "code", None),
        P("head", "code"),
        P("head", "code", None),
    )
    return jax.shard_map(
        shards,
        mesh=mesh,
        in_specs=placed,
        out_specs=(P(("head", "code"), None), P("head", "code"), P("head", "code", None)),
        check_vma=False,
    )
```
